256 devices in a mesh: dp: 8 (over x, core), ctx: 32 (over z, y).
Axes of the slice: x: 4, y: 4, z: 8, core: 2. Of those that a mesh axis runs over, the one named last changes fastest.
Arguments:
- hidden: bfloat16 [8, 4096, 8192], P('dp', 'ctx'), may hold values from -6 to 6
- queries: bfloat16 [8, 4096, 4096], P('dp', 'ctx'), may hold values from -48 to 48
- keys: bfloat16 [8, 4096, 512], P('dp', 'ctx'), may hold values from -5 to 5
- adapter_down_factor: bfloat16 [8192, 64], replicated, may hold values from -0.0625 to 0.0625
- adapter_up_factor: bfloat16 [64, 512], replicated, may hold values from -0.75 to 0.75
- down_direction: bfloat16 [8192, 64], replicated, may hold values from -0.59765625 to 0.59765625
- up_direction: bfloat16 [64, 512], replicated, may hold values from -6 to 6
- trajectory_window_index: int32 [8], P('dp'), may hold values from 0 to 3
- lengths: int32 [8], P('dp'), may hold values from 1024 to 17407, as said below
Outputs:
- fisher_down: float32 [8192, 64], P('ctx')
- fisher_up: float32 [64, 512], P(None, 'ctx')
- curvature: float32 [], replicated
The draws below stay inside these ranges and needn't reach their ends.
Inputs may be any that keep to these rules, and one draw needn't show every extreme that they name: lengths[b] - 4096 * trajectory_window_index[b] lies between a quarter and five quarters of 4096.
All inputs are finite; a program needn't handle non-finite values.
Results may differ from the reference program's by a relative error of at most 0.0059.
Values may be sent and summed in bfloat16 or wider, within the bound.
A program may use at most 64 MiB of HBM per device.

```python
import math
import jax
import jax.numpy as jnp
from jax import lax

MODEL_WIDTH = 8192
HEAD_WIDTH = 128
GROUP = 8
ADAPTER_RANK = 64
HEADS = 32
KEY_VALUE_HEADS = 4
SPAN = 4096
TRAJ = 8


def window_pair(key):
    index_draw = jax.random.randint(jax.random.fold_in(key, 21), (TRAJ,), 0, 4)
    extra_draw = jax.random.randint(jax.random.fold_in(key, 22), (TRAJ,), SPAN // 4, SPAN + SPAN // 4)
    order = jax.random.permutation(jax.random.fold_in(key, 23), TRAJ)
    slots = jnp.arange(TRAJ, dtype=jnp.int32)
    top_slot = slots == order[0]
    low_slot = slots == order[1]
    index_draw = jnp.where(top_slot, 3, jnp.where(low_slot, 0, index_draw))
    extra_draw = jnp.where(top_slot, SPAN + SPAN // 4 - 1, jnp.where(low_slot, SPAN // 4, extra_draw))
    return (index_draw, index_draw * SPAN + extra_draw)


def draw_trajectory_window_index(key, part):
    return window_pair(key)[0].astype(jnp.int32)


def draw_lengths(key, part):
    return window_pair(key)[1].astype(jnp.int32)


def key_field(key):
    field_key = jax.random.fold_in(key, 11)
    bell_part = jnp.clip(jax.random.normal(field_key, (TRAJ, SPAN, KEY_VALUE_HEADS * HEAD_WIDTH), jnp.float32), -5.0, 5.0)
    return bell_part


def draw_keys(key, part):
    shared_field = key_field(key)
    key = jax.random.fold_in(key, 3)
    own_noise = jax.random.normal(key, (TRAJ, SPAN, KEY_VALUE_HEADS * HEAD_WIDTH), jnp.float32)
    return jnp.clip(0.95 * shared_field + 0.3 * own_noise, -5.0, 5.0).astype(jnp.bfloat16)


def draw_queries(key, part):
    key = jax.random.fold_in(key, 1)
    query_key = jax.random.fold_in(key, 0)
    drawn = jnp.clip(jax.random.normal(query_key, (TRAJ, SPAN, HEADS * HEAD_WIDTH), jnp.float32), -5.0, 5.0)
    return drawn.astype(jnp.bfloat16)


def levels(key, shape, pieces, least, largest):
    gain, own = 1.0, jax.random.fold_in(key, 6)
    for position, blocks in pieces:
        draws = jnp.exp(jax.random.uniform(jax.random.fold_in(own, position), (blocks,), jnp.float32, least / len(pieces), largest / len(pieces)))
        gain = gain * jnp.repeat(draws, shape[position] // blocks).reshape([-1 if axis == position else 1 for axis in range(len(shape))])
    return gain


def centred(own_key, extent, width, reach, cuts=(), kind=jnp.bfloat16):
    values = width * jax.random.normal(own_key, extent, jnp.float32)
    if cuts:
        values = values * levels(own_key, extent, cuts, -0.22, 0.18)
    return jnp.clip(values, -reach, reach).astype(kind)


def setup_inputs(seed: int = 0) -> dict:
    seeds = jax.random.split(jax.random.key(seed), 10)
    hidden = centred(seeds[0], (TRAJ, SPAN, MODEL_WIDTH), 1.0, 6.0, ((0, 8), (1, 32)))
    queries = draw_queries(jax.random.fold_in(seeds[9], 71), 0)
    keys = draw_keys(jax.random.fold_in(seeds[9], 71), 0)
    adapter_down_factor = centred(seeds[3], (MODEL_WIDTH, ADAPTER_RANK), MODEL_WIDTH ** -0.5, 0.0625)
    adapter_up_factor = centred(seeds[4], (ADAPTER_RANK, KEY_VALUE_HEADS * HEAD_WIDTH), ADAPTER_RANK ** -0.5, 0.75)
    down_direction = centred(seeds[5], (MODEL_WIDTH, ADAPTER_RANK), 0.1, 0.59765625)
    up_direction = centred(seeds[6], (ADAPTER_RANK, KEY_VALUE_HEADS * HEAD_WIDTH), 1.0, 6.0)
    trajectory_window_index = draw_trajectory_window_index(jax.random.fold_in(seeds[9], 71), 0)
    lengths = draw_lengths(jax.random.fold_in(seeds[9], 71), 0)
    return {"hidden": hidden, "queries": queries, "keys": keys, "adapter_down_factor": adapter_down_factor, "adapter_up_factor": adapter_up_factor, "down_direction": down_direction, "up_direction": up_direction, "trajectory_window_index": trajectory_window_index, "lengths": lengths}


def rotate(values, positions, head_count, head_size):
    half_size = head_size // 2
    inv_freq = jnp.exp(jnp.arange(half_size, dtype=jnp.float32) * (-2.0 * math.log(1000000.0) / head_size))
    angles = positions.astype(jnp.float32)[..., None] * inv_freq
    cosine = jnp.cos(angles)[..., None, :]
    sine_part = jnp.sin(angles)[..., None, :]
    lead_shape = values.shape[:-1]
    as_heads = values.astype(jnp.float32).reshape(lead_shape + (head_count, head_size))
    lower_half = as_heads[..., :half_size]
    upper_half = as_heads[..., half_size:]
    turned = jnp.concatenate([lower_half * cosine - upper_half * sine_part, upper_half * cosine + lower_half * sine_part], axis=-1)
    return turned.reshape(values.shape).astype(jnp.bfloat16)

def matrix_product(left, right):
    return jnp.dot(left, right, preferred_element_type=jnp.float32)

def attend_ref(query_rows, key_rows, tangent_rows, valid_rows):
    span_len = query_rows.shape[0]
    block_rows = math.gcd(span_len, 512)
    score_scale = 1.0 / math.sqrt(query_rows.shape[1])
    columns = jnp.arange(span_len, dtype=jnp.int32)
    keys_f = key_rows.astype(jnp.float32)
    tangent_f = tangent_rows.astype(jnp.float32)

    def block_step(block_index, carry_in):
        grad_sum, curvature_sum = carry_in
        row_start = block_index * block_rows
        query_block = lax.dynamic_slice_in_dim(query_rows, row_start, block_rows, 0).astype(jnp.float32)
        scores = jnp.einsum('qd,kd->qk', query_block, keys_f, precision=lax.Precision.HIGHEST) * score_scale
        causal = columns[None, :] <= (row_start + jnp.arange(block_rows, dtype=jnp.int32))[:, None]
        scores = jnp.where(causal, scores, -jnp.inf)
        row_max = lax.optimization_barrier(jnp.max(scores, axis=1, keepdims=True))
        weights = jnp.exp(scores - row_max)
        probs_bf = (weights / lax.optimization_barrier(jnp.sum(weights, axis=1, keepdims=True))).astype(jnp.bfloat16)
        probs_f = probs_bf.astype(jnp.float32)
        out_tangent = jnp.einsum('qk,kd->qd', probs_f, tangent_f, precision=lax.Precision.HIGHEST)
        keep_rows = lax.dynamic_slice_in_dim(valid_rows, row_start, block_rows, 0)[:, None]
        cotangent = (out_tangent * keep_rows).astype(jnp.bfloat16).astype(jnp.float32)
        grad_sum = grad_sum + jnp.einsum('qk,qd->kd', probs_f, cotangent, precision=lax.Precision.HIGHEST)
        curvature_sum = curvature_sum + jnp.sum(keep_rows * out_tangent * out_tangent)
        return (grad_sum, curvature_sum)
    init_carry = (jnp.zeros((span_len, query_rows.shape[1]), jnp.float32), jnp.zeros((), jnp.float32))
    grad_sum, curvature_sum = lax.fori_loop(0, span_len // block_rows, block_step, init_carry)
    return (grad_sum.astype(jnp.bfloat16), curvature_sum)

def reference(hidden, queries, keys, adapter_down_factor, adapter_up_factor, down_direction, up_direction, trajectory_window_index, lengths):
    positions = trajectory_window_index[:, None] * SPAN + jnp.arange(SPAN, dtype=jnp.int32)[None, :]
    valid_all = (positions < lengths[:, None]).astype(jnp.float32)
    rot_query = rotate(queries, positions, HEADS, HEAD_WIDTH)
    rot_keys = rotate(keys, positions, KEY_VALUE_HEADS, HEAD_WIDTH)
    kv_of_head = jnp.arange(HEADS, dtype=jnp.int32) // GROUP

    def per_traj(carry_in, inputs):
        hidden_state_rows, query_rows, key_rows, valid_rows = inputs
        down_activation = matrix_product(hidden_state_rows, adapter_down_factor).astype(jnp.bfloat16)
        down_direction_rows = matrix_product(hidden_state_rows, down_direction).astype(jnp.bfloat16)
        value_direction = (matrix_product(down_direction_rows, adapter_up_factor) + matrix_product(down_activation, up_direction)).astype(jnp.bfloat16)
        head_query = query_rows.reshape(SPAN, HEADS, HEAD_WIDTH).transpose(1, 0, 2)

        def per_head(item):
            one_query, kv_index = item
            one_keys = lax.dynamic_slice_in_dim(key_rows, kv_index * HEAD_WIDTH, HEAD_WIDTH, 1)
            one_tangent = lax.dynamic_slice_in_dim(value_direction, kv_index * HEAD_WIDTH, HEAD_WIDTH, 1)
            return attend_ref(one_query, one_keys, one_tangent, valid_rows)
        head_grads, head_curv = lax.map(per_head, (head_query, kv_of_head))
        value_gradient = lax.optimization_barrier(jnp.sum(head_grads.astype(jnp.float32).reshape(KEY_VALUE_HEADS, GROUP, SPAN, HEAD_WIDTH), axis=1))
        value_gradient = value_gradient.astype(jnp.bfloat16).transpose(1, 0, 2).reshape(SPAN, KEY_VALUE_HEADS * HEAD_WIDTH)
        mixed_rank_rows = matrix_product(value_gradient, adapter_up_factor.T).astype(jnp.bfloat16)
        down_sum = carry_in[0] + matrix_product(hidden_state_rows.T, mixed_rank_rows)
        up_sum = carry_in[1] + matrix_product(down_activation.T, value_gradient)
        curv_sum = carry_in[2] + jnp.sum(head_curv)
        return ((down_sum, up_sum, curv_sum), None)
    init_carry = (jnp.zeros((MODEL_WIDTH, ADAPTER_RANK), jnp.float32), jnp.zeros((ADAPTER_RANK, KEY_VALUE_HEADS * HEAD_WIDTH), jnp.float32), jnp.zeros((), jnp.float32))
    (down_sum, up_sum, curv_sum), unused = lax.scan(per_traj, init_carry, (hidden, rot_query, rot_keys, valid_all))
    count = jnp.sum(valid_all)
    tangent_sq = jnp.sum(jnp.square(down_direction.astype(jnp.float32))) + jnp.sum(jnp.square(up_direction.astype(jnp.float32)))
    rescale = tangent_sq / (curv_sum + 1e-06)
    return (down_sum * rescale, up_sum * rescale, curv_sum / count)
```

```python
import functools
import math

import jax
import jax.numpy as jnp
from jax import lax
from jax.experimental import pallas as pl
from jax.experimental.pallas import tpu as pltpu
from jax.sharding import PartitionSpec as P

HW = 128
GROUP = 8
RANK = 64
NZ, NY, NX = 8, 4, 4
ROWS = 256
CHUNK = 2048
F32 = jnp.float32
BF = jnp.bfloat16
MESH = pl.DeviceIdType.MESH
NN = (((1,), (0,)), ((), ()))
NT = (((1,), (1,)), ((), ()))
VM = pl.BlockSpec(memory_space=pltpu.VMEM)
SM = pl.BlockSpec(memory_space=pltpu.SMEM)


def dot(a, b, dims=NN):
    return lax.dot_general(a, b, dims, preferred_element_type=F32)


def place():
    ctx = lax.axis_index("ctx")
    return ctx // NY, lax.rem(ctx, NY)


class Flow:
    def __init__(self, index, size, here, block, peer, send_sem, recv_sem):
        self.index, self.size, self.here = index, size, here
        self.block, self.peer = block, peer
        self.send_sem, self.recv_sem = send_sem, recv_sem
        self.step, self.sent = 0, []

    def copy(self, step, way, origin):
        half = None if step < self.size // 2 else way
        ref = self.block(lax.rem(origin + 2 * self.size, self.size), half)
        to = lax.rem(self.here + (1 if way == 0 else self.size - 1), self.size)
        return pltpu.make_async_remote_copy(
            src_ref=ref,
            dst_ref=ref,
            send_sem=self.send_sem.at[self.index, step - 1, way],
            recv_sem=self.recv_sem.at[self.index, step - 1, way],
            device_id=self.peer(to),
            device_id_type=MESH,
        )

    def send(self):
        self.step += 1
        for way, sign in ((0, -1), (1, 1)):
            copy = self.copy(self.step, way, self.here + sign * (self.step - 1))
            copy.start()
            self.sent.append(copy)

    def receive(self):
        for way, sign in ((0, -1), (1, 1)):
            self.copy(self.step, way, self.here + sign * self.step).wait_recv()

    def last(self):
        return self.step == self.size // 2


def gather_kernel(hidden, queries, keys, down, direction, cosine, sine, gath, qT, send_sem, recv_sem):
    z, y = place()
    barrier = pltpu.get_barrier_semaphore()

    def at(zz, yy):
        return {"ctx": zz * NY + yy}

    def ring(value, size):
        return lax.rem(value + size, size)

    for target in (
        at(z, ring(y + 1, NY)),
        at(z, ring(y - 1, NY)),
        at(ring(z + 1, NZ), y),
        at(ring(z - 1, NZ), y),
    ):
        pl.semaphore_signal(barrier, inc=1, device_id=target, device_id_type=MESH)

    cos, sin = cosine[...], sine[...]

    def turn(u):
        u = u.astype(F32)
        return u * cos + pltpu.roll(u, HW // 2, 1) * sin

    for g in range(4):
        gath[g, z, y] = turn(keys[:, g * HW : (g + 1) * HW]).astype(BF)
    gath[4, z, y, 0:RANK, :] = dot(down[...], hidden[...], NT).astype(BF)
    gath[4, z, y, RANK:HW, :] = dot(direction[...], hidden[...], NT).astype(BF)
    pl.semaphore_wait(barrier, 4)

    parts = (slice(3, 5), slice(0, 3))

    def cut(ref, half):
        if half is None:
            return ref
        return ref.at[:, half * 64 : half * 64 + 64, :]

    count = [0]

    def make_y(part, zz):
        count[0] += 1
        return Flow(
            count[0] - 1, NY, y,
            lambda origin, half: cut(gath.at[part, zz, origin], half),
            lambda to: at(z, to), send_sem, recv_sem,
        )

    def make_z(part, yy):
        count[0] += 1
        return Flow(
            count[0] - 1, NZ, z,
            lambda origin, half: cut(gath.at[part, origin, yy], half),
            lambda to: at(to, y), send_sem, recv_sem,
        )

    first_y = make_y(parts[0], z)
    first_z = make_z(parts[1], y)
    flows, done = [first_y, first_z], []
    flows.append(make_z(parts[0], y))
    flows.append(make_y(parts[1], z))
    for flow in flows:
        flow.send()

    scale = math.log2(math.e) / math.sqrt(HW)

    def rotate_queries(i, _):
        for h in range(ROWS // HW):
            u = queries[:, pl.ds(pl.multiple_of(i * ROWS + h * HW, HW), HW)]
            qT[i, :, h * HW : (h + 1) * HW] = jnp.transpose(turn(u) * scale).astype(BF)
        return 0

    lax.fori_loop(0, qT.shape[0], rotate_queries, 0)

    while flows:
        fresh = []
        for flow in list(flows):
            flow.receive()
            step = flow.step
            if flow.last():
                flows.remove(flow)
                done.append(flow)
            else:
                flow.send()
            near = (step,) if step == flow.size // 2 else (-step, step)
            if flow is first_y:
                fresh += [make_z(parts[0], ring(y + o, NY)) for o in near]
            if flow is first_z:
                fresh += [make_y(parts[1], ring(z + o, NZ)) for o in near]
        for flow in fresh:
            flow.send()
        flows += fresh
    for flow in done:
        for copy in flow.sent:
            copy.wait_send()


def gather(hidden, queries, keys, down, direction, cosine, sine):
    return pl.pallas_call(
        gather_kernel,
        out_shape=(
            jax.ShapeDtypeStruct((5, NZ, NY, HW, HW), BF),
            jax.ShapeDtypeStruct((queries.shape[1] // ROWS, HW, ROWS), BF),
        ),
        in_specs=[VM] * 7,
        out_specs=(VM, VM),
        scratch_shapes=[
            pltpu.SemaphoreType.DMA((14, 4, 2)),
            pltpu.SemaphoreType.DMA((14, 4, 2)),
        ],
        compiler_params=pltpu.CompilerParams(
            collective_id=0, has_side_effects=True, vmem_limit_bytes=48 * 1024 * 1024
        ),
    )(hidden, queries, keys, down, direction, cosine, sine)


def attend_kernel(
    info, gath, qT, wT, up, mixed_ref, upT_ref, curv_ref, s_buf, p_buf, vT, grad, oacc, w_buf, curv_acc
):
    kvh = 4
    blocks = NZ * NY
    span = blocks * HW
    per = CHUNK // HW
    me, live = info[0], info[1]
    chunks = lax.div(me, per) + 1
    per_g = GROUP * HW // ROWS
    total = kvh * per_g

    def tangents(j, _):
        for b in range(per):
            vv = dot(wT[...], gath[4, j * per + b]).astype(BF)
            for g in range(kvh):
                vT[g, 0:HW, pl.ds(pl.multiple_of(j * CHUNK + b * HW, HW), HW)] = vv[g * HW : (g + 1) * HW]
        return 0

    lax.fori_loop(0, chunks, tangents, 0)
    ones = jnp.where(lax.broadcasted_iota(jnp.int32, (16, span), 0) == 0, 1.0, 0.0).astype(BF)
    for g in range(kvh):
        vT[g, HW : HW + 16, :] = ones
    grad[...] = jnp.zeros_like(grad)
    curv_acc[...] = jnp.zeros_like(curv_acc)
    qpos = me * HW + lax.rem(lax.broadcasted_iota(jnp.int32, (1, ROWS), 1), HW)
    liverow = (qpos < live).astype(F32)

    def step(i, score, weigh, back, m_prev):
        even, odd = lax.rem(i, 2), lax.rem(i + 1, 2)
        if weigh:
            oacc[...] = jnp.zeros_like(oacc)
        q = qT[i] if score else None

        def body(j, mx):
            ks = pl.multiple_of(j * CHUNK, CHUNK)
            if back:
                grad[lax.div(i - 2, per_g), :, pl.ds(ks, CHUNK)] += dot(
                    w_buf[even], p_buf[even, pl.ds(ks, CHUNK), :], NT
                )
            if weigh:
                p = jnp.exp2(s_buf[odd, pl.ds(ks, CHUNK), :] - m_prev).astype(BF)
                p_buf[odd, pl.ds(ks, CHUNK), :] = p
                oacc[...] += dot(vT[lax.div(i - 1, per_g), :, pl.ds(ks, CHUNK)], p)
            if score:
                kc = gath[lax.div(i, per_g), pl.ds(j * per, per)].reshape(CHUNK, HW)
                s = dot(kc, q)
                kpos = ks + lax.broadcasted_iota(jnp.int32, (CHUNK, ROWS), 0)
                s = jnp.where(kpos <= qpos, s, -1e30)
                s_buf[even, pl.ds(ks, CHUNK), :] = s
                mx = jnp.maximum(mx, jnp.max(s.reshape(CHUNK // 8, 8, ROWS), axis=0))
            return mx

        mx = lax.fori_loop(0, chunks, body, jnp.full((8, ROWS), -1e30, F32))
        if weigh:
            o = oacc[...]
            inv = 1.0 / o[HW : HW + 1]
            out = o[0:HW] * inv * liverow
            curv_acc[...] += jnp.sum((out * out).reshape(HW // 8, 8, ROWS), axis=0)
            w_buf[odd] = (out * inv).astype(BF)
        return jnp.max(mx, axis=0, keepdims=True)

    top = step(0, True, False, False, None)
    top = step(1, True, True, False, top)
    top = lax.fori_loop(2, total, lambda i, m: step(i, True, True, True, m), top)
    step(total, False, True, True, top)
    step(total + 1, False, False, True, None)

    mixed_ref[...] = jnp.zeros_like(mixed_ref)
    upT_ref[...] = jnp.zeros_like(upT_ref)

    def finish(j, _):
        ks = pl.multiple_of(j * CHUNK, CHUNK)
        grads = [grad[g, :, pl.ds(ks, CHUNK)].astype(BF) for g in range(kvh)]
        mixed = sum(dot(up[:, g * HW : (g + 1) * HW], grads[g]) for g in range(kvh)).astype(BF)
        for b in range(per):
            cols = slice(b * HW, (b + 1) * HW)
            mixed_ref[j * per + b] = mixed[:, cols]
            act = gath[4, j * per + b, 0:RANK, :]
            for g in range(kvh):
                upT_ref[g * HW : (g + 1) * HW, :] += dot(grads[g][:, cols], act, NT)
        return 0

    lax.fori_loop(0, chunks, finish, 0)
    both = curv_acc[:, 0:HW] + curv_acc[:, HW : 2 * HW]
    row = lax.broadcasted_iota(jnp.int32, (8, HW), 0)
    lane = lax.broadcasted_iota(jnp.int32, (8, HW), 1)
    mine = ((me * HW + lane) < live).astype(F32)
    curv_ref[...] = jnp.where(
        row == 0, jnp.sum(both, axis=0, keepdims=True), jnp.where(row == 1, mine, 0.0)
    )


def attention(info, gath, qT, wT, up):
    span = NZ * NY * HW
    return pl.pallas_call(
        attend_kernel,
        out_shape=(
            jax.ShapeDtypeStruct((NZ * NY, RANK, HW), BF),
            jax.ShapeDtypeStruct((4 * HW, RANK), F32),
            jax.ShapeDtypeStruct((8, HW), F32),
        ),
        in_specs=[SM, VM, VM, VM, VM],
        out_specs=(VM, VM, VM),
        scratch_shapes=[
            pltpu.VMEM((2, span, ROWS), F32),
            pltpu.VMEM((2, span, ROWS), BF),
            pltpu.VMEM((4, HW + 16, span), BF),
            pltpu.VMEM((4, HW, span), F32),
            pltpu.VMEM((HW + 16, ROWS), F32),
            pltpu.VMEM((2, HW, ROWS), BF),
            pltpu.VMEM((8, ROWS), F32),
        ],
        compiler_params=pltpu.CompilerParams(vmem_limit_bytes=56 * 1024 * 1024),
    )(info, gath, qT, wT, up)


def reduce_kernel(
    mixed, upT, curv, hidden, direction, up_direction, down_out, up_out, curv_out,
    got_y, sum_y, got_z, part, got_core, sum_core, got_x, sum_x, ups, got_dy, got_uy, sum_dy, got_dz, all_dp,
    send_sem, recv_sem,
):
    z, y = place()
    ctx = lax.axis_index("ctx")
    dp = lax.axis_index("dp")
    x, core = dp // 2, lax.rem(dp, 2)
    barrier = pltpu.get_barrier_semaphore()

    def at_y(o):
        return {"ctx": z * NY + lax.rem(y + o, NY)}

    def at_z(o):
        return {"ctx": lax.rem(z + o, NZ) * NY + y}

    def at_dp(o):
        return {"dp": lax.rem(dp + o, 8)}

    for o in range(1, NY):
        pl.semaphore_signal(barrier, inc=1, device_id=at_y(o), device_id_type=MESH)
    for o in range(1, NZ):
        pl.semaphore_signal(barrier, inc=1, device_id=at_z(o), device_id_type=MESH)
    for o in range(1, 8):
        pl.semaphore_signal(barrier, inc=1, device_id=at_dp(o), device_id_type=MESH)

    used = [0]
    sent = []

    def send(src, dst, to):
        copy = pltpu.make_async_remote_copy(
            src_ref=src, dst_ref=dst, send_sem=send_sem.at[used[0]], recv_sem=recv_sem.at[used[0]],
            device_id=to, device_id_type=MESH,
        )
        used[0] += 1
        copy.start()
        sent.append(copy)
        return copy

    pl.semaphore_wait(barrier, 17)

    copies = [
        send(mixed.at[:, lax.rem(y + o, NY)], got_y.at[o - 1], at_y(o)) for o in range(1, NY)
    ]
    for i in range(32):
        block = upT[16 * i : 16 * i + 16, :]
        ups[i % NY, i // NY] = jnp.concatenate([block[0:8], block[8:16]], axis=1)
    for i in range(NY):
        ups[i, NZ] = curv[...]

    def squares(i, acc):
        d = direction[:, pl.ds(pl.multiple_of(i * 512, 512), 512)].astype(F32)
        return acc + jnp.sum((d * d).reshape(8, 8, 512), axis=0)

    squared = jnp.sum(lax.fori_loop(0, 16, squares, jnp.zeros((8, 512), F32)))
    ud = up_direction[...].astype(F32)
    squared = squared + jnp.sum(ud * ud)

    for copy in copies:
        copy.wait_recv()

    def add_y(i, _):
        acc = mixed[i, y].astype(F32)
        for o in range(NY - 1):
            acc = acc + got_y[o, i].astype(F32)
        sum_y[i] = acc.astype(BF)
        return 0

    lax.fori_loop(0, NZ, add_y, 0)
    copies = [
        send(sum_y.at[lax.rem(z + o, NZ)], got_z.at[o - 1], at_z(o)) for o in range(1, NZ)
    ]
    for copy in copies:
        copy.wait_recv()
    own = sum_y[z].astype(F32)
    for o in range(NZ - 1):
        own = own + got_z[o].astype(F32)
    own = own.astype(BF)

    def down(i, _):
        d = dot(own, hidden[:, pl.ds(pl.multiple_of(i * 256, 256), 256)])
        for r in range(8):
            rows = d[8 * r : 8 * r + 8]
            part[r // 2, r % 2, i] = jnp.concatenate([rows[:, 0:HW], rows[:, HW:]], axis=0).astype(BF)
        return 0

    lax.fori_loop(0, 32, down, 0)

    copy = send(part.at[:, 1 - core], got_core, {"dp": x * 2 + 1 - core})
    copy.wait_recv()

    def add_core(i, _):
        for xx in range(NX):
            sum_core[xx, i] = (part[xx, core, i].astype(F32) + got_core[xx, i].astype(F32)).astype(BF)
        return 0

    lax.fori_loop(0, 32, add_core, 0)
    copies = [
        send(sum_core.at[lax.rem(x + o, NX)], got_x.at[o - 1], {"dp": lax.rem(x + o, NX) * 2 + core})
        for o in range(1, NX)
    ]
    for copy in copies:
        copy.wait_recv()

    def add_x(i, _):
        for yy in range(NY):
            acc = sum_core[x, i * NY + yy].astype(F32)
            for o in range(NX - 1):
                acc = acc + got_x[o, i * NY + yy].astype(F32)
            sum_x[yy, i] = acc.astype(BF)
        return 0

    lax.fori_loop(0, NZ, add_x, 0)
    copies = []
    for o in range(1, NY):
        to = lax.rem(y + o, NY)
        copies.append(send(sum_x.at[to], got_dy.at[o - 1], at_y(o)))
        copies.append(send(ups.at[to], got_uy.at[o - 1], at_y(o)))
    for copy in copies:
        copy.wait_recv()
    scal = ups[y, NZ]
    for o in range(NY - 1):
        scal = scal + got_uy[o, NZ]
    for i in range(NZ):
        acc = sum_x[y, i].astype(F32)
        upa = ups[y, i]
        for o in range(NY - 1):
            acc = acc + got_dy[o, i].astype(F32)
            upa = upa + got_uy[o, i]
        sum_dy[i, 0:16] = acc
        sum_dy[i, 16:24] = upa
        sum_dy[i, 24:32] = scal
    copies = [
        send(sum_dy.at[lax.rem(z + o, NZ)], got_dz.at[o - 1], at_z(o)) for o in range(1, NZ)
    ]
    for copy in copies:
        copy.wait_recv()
    acc = sum_dy[z]
    for o in range(NZ - 1):
        acc = acc + got_dz[o]
    all_dp[dp] = acc
    copies = [send(all_dp.at[dp], all_dp.at[dp], at_dp(o)) for o in range(1, 8)]
    for o in range(1, 8):
        slot = lax.rem(dp + 8 - o, 8)
        base = used[0] - 7 + o - 1
        pltpu.make_async_remote_copy(
            src_ref=all_dp.at[slot], dst_ref=all_dp.at[slot], send_sem=send_sem.at[base],
            recv_sem=recv_sem.at[base], device_id=at_dp(o), device_id_type=MESH,
        ).wait_recv()
    tail = all_dp[0, 16:32]
    for r in range(1, 8):
        tail = tail + all_dp[r, 16:32]
    curv_sum = jnp.sum(tail[8:9])
    count = jnp.sum(tail[9:10])
    rescale = squared / (curv_sum + 1e-06)
    for r in range(8):
        down_out[8 * r : 8 * r + 8, 0:HW] = all_dp[r, 0:8] * rescale
        down_out[8 * r : 8 * r + 8, HW : 2 * HW] = all_dp[r, 8:16] * rescale
    up_out[0:8, :] = tail[0:8, 0:RANK] * rescale
    up_out[8:16, :] = tail[0:8, RANK:HW] * rescale
    curv_out[...] = jnp.full((8, HW), curv_sum / count, F32)
    for copy in sent:
        copy.wait_send()


def reduce(mixed, upT, curv, hidden, direction, up_direction):
    return pl.pallas_call(
        reduce_kernel,
        out_shape=(
            jax.ShapeDtypeStruct((RANK, 256), F32),
            jax.ShapeDtypeStruct((16, RANK), F32),
            jax.ShapeDtypeStruct((8, HW), F32),
        ),
        in_specs=[VM] * 6,
        out_specs=(VM, VM, VM),
        scratch_shapes=[
            pltpu.VMEM((NY - 1, NZ, RANK, HW), BF),
            pltpu.VMEM((NZ, RANK, HW), BF),
            pltpu.VMEM((NZ - 1, RANK, HW), BF),
            pltpu.VMEM((NX, 2, 32, 16, HW), BF),
            pltpu.VMEM((NX, 32, 16, HW), BF),
            pltpu.VMEM((NX, 32, 16, HW), BF),
            pltpu.VMEM((NX - 1, 32, 16, HW), BF),
            pltpu.VMEM((NY, NZ, 16, HW), BF),
            pltpu.VMEM((NY, NZ + 1, 8, HW), F32),
            pltpu.VMEM((NY - 1, NZ, 16, HW), BF),
            pltpu.VMEM((NY - 1, NZ + 1, 8, HW), F32),
            pltpu.VMEM((NZ, 32, HW), F32),
            pltpu.VMEM((NZ - 1, 32, HW), F32),
            pltpu.VMEM((8, 32, HW), F32),
            pltpu.SemaphoreType.DMA((40,)),
            pltpu.SemaphoreType.DMA((40,)),
        ],
        compiler_params=pltpu.CompilerParams(
            collective_id=1, has_side_effects=True, vmem_limit_bytes=48 * 1024 * 1024
        ),
    )(mixed, upT, curv, hidden, direction, up_direction)


def body(hidden, queries, keys, down, up, direction, up_direction, window, lengths):
    seq = hidden.shape[1]
    span = seq * NZ * NY
    ctx = lax.axis_index("ctx")
    position = window[0] * span + ctx * seq + jnp.arange(seq, dtype=jnp.int32)
    inv_freq = jnp.exp(jnp.arange(HW // 2, dtype=F32) * (-2.0 * math.log(1000000.0) / HW))
    angles = position.astype(F32)[:, None] * inv_freq
    cosine, sine = jnp.cos(angles), jnp.sin(angles)
    cosine = jnp.concatenate([cosine, cosine], axis=1)
    sine = jnp.concatenate([-sine, sine], axis=1)
    info = jnp.stack([ctx.astype(jnp.int32), lengths[0] - window[0] * span])
    wT = jnp.concatenate([up_direction, up], axis=0).T
    gath, qT = gather(hidden[0], queries[0], keys[0], down.T, direction.T, cosine, sine)
    mixed, upT, curv = attention(info, gath.reshape(5, NZ * NY, HW, HW), qT, wT, up)
    down_out, up_out, curv_out = reduce(
        mixed.reshape(NZ, NY, RANK, HW), upT, curv, hidden[0], direction.T, up_direction
    )
    return down_out.T, up_out.T, curv_out[0, 0]


def solution(mesh):
    placed = (
        P("dp", "ctx", None),
        P("dp", "ctx", None),
        P("dp", "ctx", None),
        P(),
        P(),
        P(),
        P(),
        P("dp"),
        P("dp"),
    )
    return jax.shard_map(
        body,
        mesh=mesh,
        in_specs=placed,
        out_specs=(P("ctx", None), P(None, "ctx"), P()),
        check_vma=False,
    )
```

```python
import functools
import math

import jax
import jax.numpy as jnp
from jax import lax
from jax.experimental import pallas as pl
from jax.experimental.pallas import tpu as pltpu
from jax.sharding import PartitionSpec as P

HW = 128
GROUP = 8
RANK = 64
NZ, NY, NX = 8, 4, 4
ROWS = 256
CHUNK = 2048
SUB = 256
F32 = jnp.float32
BF = jnp.bfloat16
MESH = pl.DeviceIdType.MESH
NN = (((1,), (0,)), ((), ()))
NT = (((1,), (1,)), ((), ()))
VM = pl.BlockSpec(memory_space=pltpu.VMEM)
SM = pl.BlockSpec(memory_space=pltpu.SMEM)


def dot(a, b, dims=NN):
    return lax.dot_general(a, b, dims, preferred_element_type=F32)


def place():
    ctx = lax.axis_index("ctx")
    return ctx // NY, lax.rem(ctx, NY)


class Flow:
    def __init__(self, index, size, here, block, peer, sems):
        self.index, self.size, self.here = index, size, here
        self.block, self.peer = block, peer
        self.send_sem, self.recv_sem = sems
        self.step = 0

    def copy(self, step, way, offset):
        half = None if step < self.size // 2 else way
        ref = self.block(lax.rem(self.here + offset + self.size, self.size), half)
        to = lax.rem(self.here + (1 if way == 0 else self.size - 1), self.size)
        return pltpu.make_async_remote_copy(
            src_ref=ref,
            dst_ref=ref,
            send_sem=self.send_sem.at[self.index, step - 1, way],
            recv_sem=self.recv_sem.at[self.index, step - 1, way],
            device_id=self.peer(to),
            device_id_type=MESH,
        )

    def send(self):
        self.step += 1
        for way, sign in ((0, -1), (1, 1)):
            self.copy(self.step, way, sign * (self.step - 1)).start()

    def receive(self):
        for way, sign in ((0, -1), (1, 1)):
            self.copy(self.step, way, sign * self.step).wait_recv()

    def advance(self):
        self.receive()
        if self.step == self.size // 2:
            return True
        self.send()
        return False

    def drain(self):
        for step in range(1, self.size // 2 + 1):
            for way, sign in ((0, -1), (1, 1)):
                self.copy(step, way, sign * (step - 1)).wait_send()


def cut(ref, half, axis):
    if half is None:
        return ref
    rows = pl.ds(half * 64, 64)
    return ref.at[(slice(None),) * axis + (rows,)]


def attend_kernel(
    info, hidden, queries, keys, down, direction, cosine, sine, wT, up,
    mixed_ref, upT_ref, curv_ref,
    gath, qT, s_even, s_odd, p_even, p_odd, vT, grad, oacc, w_even, w_odd, curv_acc, send_sem, recv_sem,
):
    z, y = place()
    barrier = pltpu.get_barrier_semaphore()

    def at(zz, yy):
        return {"ctx": zz * NY + yy}

    ys = [lax.rem(y + o, NY) for o in range(NY)]
    zs = [lax.rem(z + o, NZ) for o in range(NZ)]
    for target in (at(z, ys[1]), at(z, ys[3]), at(zs[1], y), at(zs[7], y)):
        pl.semaphore_signal(barrier, inc=1, device_id=target, device_id_type=MESH)

    cos, sin = cosine[...], sine[...]

    def turn(u):
        u = u.astype(F32)
        return u * cos + pltpu.roll(u, HW // 2, 1) * sin

    gath[0, z, y, 0:RANK, :] = dot(down[...], hidden[...], NT).astype(BF)
    gath[0, z, y, RANK:HW, :] = dot(direction[...], hidden[...], NT).astype(BF)
    for g in range(4):
        gath[1 + g, z, y] = turn(keys[:, g * HW : (g + 1) * HW]).astype(BF)
    pl.semaphore_wait(barrier, 4)

    made = []
    sems = (send_sem, recv_sem)

    def ring_y(part, zz):
        flow = Flow(len(made), NY, y, lambda o, half: cut(gath.at[part, zz, o], half, 0), lambda to: at(z, to), sems)
        made.append(flow)
        return flow

    def ring_z(part, yy):
        flow = Flow(len(made), NZ, z, lambda o, half: cut(gath.at[part, o, yy], half, 0), lambda to: at(to, y), sems)
        made.append(flow)
        return flow

    def ring_z_all(part):
        flow = Flow(
            len(made), NZ, z, lambda o, half: cut(gath.at[part, o], half, 1), lambda to: at(to, y), sems
        )
        made.append(flow)
        return flow

    def ring_z_pair(part):
        flow = Flow(
            len(made), NZ, z, lambda o, half: cut(gath.at[part, o, y], half, 1), lambda to: at(to, y), sems
        )
        made.append(flow)
        return flow

    def ring_y_all(part):
        flow = Flow(
            len(made), NY, y, lambda o, half: cut(gath.at[part, :, o], half, 2), lambda to: at(z, to), sems
        )
        made.append(flow)
        return flow

    first_y, first_z = ring_y(0, z), ring_z(1, y)
    lanes = [ring_z(0, y), ring_y(1, z)]
    for flow in [first_y, first_z] + lanes:
        flow.send()
    heads = [first_y, first_z]

    scale = math.log2(math.e) / math.sqrt(HW)

    def rotate_queries(i, _):
        for h in range(ROWS // HW):
            u = queries[:, pl.ds(pl.multiple_of(i * ROWS + h * HW, HW), HW)]
            qT[i, :, h * HW : (h + 1) * HW] = jnp.transpose(turn(u) * scale).astype(BF)
        return 0

    lax.fori_loop(0, qT.shape[0], rotate_queries, 0)

    late = {}
    for slot in range(1, 7):
        fresh = []
        for flow in list(heads):
            end = flow.advance()
            step = flow.step if not end else flow.size // 2
            step = step if end else step - 1
            near = (step,) if end else (flow.size - step, step)
            for o in near:
                fresh.append(ring_z(0, ys[o]) if flow is first_y else ring_y(1, zs[o]))
            if end:
                heads.remove(flow)
        for flow in list(lanes):
            if flow.advance():
                lanes.remove(flow)
        for flow in fresh:
            flow.send()
        lanes += fresh
        if slot == 2:
            late["z34"] = ring_z_pair(slice(3, 5))
            late["z34"].send()
        elif slot <= 6 and "z34" in late:
            if late["z34"].advance():
                late["y34"] = ring_y_all(slice(3, 5))
                late["y34"].send()
        if slot == 3:
            late["y2"] = ring_y(2, z)
            late["y2"].send()
        elif slot in (4, 5):
            if late["y2"].advance():
                late["z2"] = ring_z_all(2)
                late["z2"].send()
        elif slot == 6:
            late["z2"].advance()

    kvh = 4
    blocks = NZ * NY
    span = blocks * HW
    per = CHUNK // HW
    me, live = z * NY + y, info[0]
    chunks = me // per + 1
    per_g = GROUP * HW // ROWS
    total = kvh * per_g
    s_bufs, p_bufs, w_bufs = (s_even, s_odd), (p_even, p_odd), (w_even, w_odd)
    zper = per // NY

    def tangents(j, _):
        for b in range(per):
            vv = dot(wT[...], gath[0, j * zper + b // NY, b % NY]).astype(BF)
            for g in range(kvh):
                vT[g, 0:HW, pl.ds(pl.multiple_of(j * CHUNK + b * HW, HW), HW)] = vv[g * HW : (g + 1) * HW]
        return 0

    lax.fori_loop(0, chunks, tangents, 0)
    ones = jnp.where(lax.broadcasted_iota(jnp.int32, (16, span), 0) == 0, 1.0, 0.0).astype(BF)
    for g in range(kvh):
        vT[g, HW : HW + 16, :] = ones
    grad[...] = jnp.zeros_like(grad)
    curv_acc[...] = jnp.zeros_like(curv_acc)
    qpos = me * HW + lax.rem(lax.broadcasted_iota(jnp.int32, (1, ROWS), 1), HW)
    liverow = (qpos < live).astype(F32)

    def step(i, even, score, weigh, back, m_prev):
        odd = 1 - even
        if weigh:
            oacc[...] = jnp.zeros_like(oacc)
        q = qT[i] if score else None

        def body(j, mx):
            o = None
            for u in range(CHUNK // SUB):
                us = pl.multiple_of(j * CHUNK + u * SUB, SUB)
                if back:
                    grad[(i - 2) // per_g, :, pl.ds(us, SUB)] += dot(
                        w_bufs[even][...], p_bufs[even][pl.ds(us, SUB), :], NT
                    )
                if score:
                    b = u * (SUB // HW)
                    kc = gath[1 + i // per_g, j * zper + b // NY, b % NY : b % NY + SUB // HW].reshape(SUB, HW)
                    s = dot(kc, q)
                    kpos = us + lax.broadcasted_iota(jnp.int32, (SUB, ROWS), 0)
                    s = jnp.where(kpos <= qpos, s, -1e30)
                    s_bufs[even][pl.ds(us, SUB), :] = s
                    mx = jnp.maximum(mx, jnp.max(s.reshape(SUB // 8, 8, ROWS), axis=0))
                if weigh:
                    p = jnp.exp2(s_bufs[odd][pl.ds(us, SUB), :] - m_prev).astype(BF)
                    p_bufs[odd][pl.ds(us, SUB), :] = p
                    t = dot(vT[(i - 1) // per_g, :, pl.ds(us, SUB)], p)
                    o = t if o is None else o + t
            if weigh:
                oacc[...] += o
            return mx

        mx = lax.fori_loop(0, chunks, body, jnp.full((8, ROWS), -1e30, F32))
        if weigh:
            o = oacc[...]
            inv = 1.0 / o[HW : HW + 1]
            out = o[0:HW] * inv * liverow
            curv_acc[...] += jnp.sum((out * out).reshape(HW // 8, 8, ROWS), axis=0)
            w_bufs[odd][...] = (out * inv).astype(BF)
        return jnp.max(mx, axis=0, keepdims=True)

    top = step(0, 0, True, False, False, None)
    late["z2"].advance()
    top = step(1, 1, True, True, False, top)
    late["z2"].advance()

    def pair(i, top):
        @pl.when(i == 2)
        def _():
            late["z2"].receive()

        @pl.when(i == 3)
        def _():
            late["y34"].step = 1
            late["y34"].advance()

        @pl.when(i == 4)
        def _():
            late["y34"].step = 2
            late["y34"].receive()

        top = step(2 * i, 0, True, True, True, top)
        return step(2 * i + 1, 1, True, True, True, top)

    top = lax.fori_loop(1, total // 2, pair, top)
    step(total, 0, False, True, True, top)
    step(total + 1, 1, False, False, True, None)

    mixed_ref[...] = jnp.zeros_like(mixed_ref)
    upT_ref[...] = jnp.zeros_like(upT_ref)

    def finish(j, _):
        ks = pl.multiple_of(j * CHUNK, CHUNK)
        grads = [grad[g, :, pl.ds(ks, CHUNK)].astype(BF) for g in range(kvh)]
        mixed = sum(dot(up[:, g * HW : (g + 1) * HW], grads[g]) for g in range(kvh)).astype(BF)
        for b in range(per):
            cols = slice(b * HW, (b + 1) * HW)
            mixed_ref[j * zper + b // NY, b % NY] = mixed[:, cols]
            act = gath[0, j * zper + b // NY, b % NY, 0:RANK, :]
            for g in range(kvh):
                upT_ref[g * HW : (g + 1) * HW, :] += dot(grads[g][:, cols], act, NT)
        return 0

    lax.fori_loop(0, chunks, finish, 0)
    both = curv_acc[:, 0:HW] + curv_acc[:, HW : 2 * HW]
    row = lax.broadcasted_iota(jnp.int32, (8, HW), 0)
    lane = lax.broadcasted_iota(jnp.int32, (8, HW), 1)
    mine = ((me * HW + lane) < live).astype(F32)
    curv_ref[...] = jnp.where(
        row == 0, jnp.sum(both, axis=0, keepdims=True), jnp.where(row == 1, mine, 0.0)
    )
    for flow in made:
        flow.drain()


def attention(info, hidden, queries, keys, down, direction, cosine, sine, wT, up):
    span = NZ * NY * HW
    return pl.pallas_call(
        attend_kernel,
        out_shape=(
            jax.ShapeDtypeStruct((NZ, NY, RANK, HW), BF),
            jax.ShapeDtypeStruct((4 * HW, RANK), F32),
            jax.ShapeDtypeStruct((8, HW), F32),
        ),
        in_specs=[SM] + [VM] * 9,
        out_specs=(VM, VM, VM),
        scratch_shapes=[
            pltpu.VMEM((5, NZ, NY, HW, HW), BF),
            pltpu.VMEM((queries.shape[1] // ROWS, HW, ROWS), BF),
            pltpu.VMEM((span, ROWS), F32),
            pltpu.VMEM((span, ROWS), F32),
            pltpu.VMEM((span, ROWS), BF),
            pltpu.VMEM((span, ROWS), BF),
            pltpu.VMEM((4, HW + 16, span), BF),
            pltpu.VMEM((4, HW, span), F32),
            pltpu.VMEM((HW + 16, ROWS), F32),
            pltpu.VMEM((HW, ROWS), BF),
            pltpu.VMEM((HW, ROWS), BF),
            pltpu.VMEM((8, ROWS), F32),
            pltpu.SemaphoreType.DMA((18, 4, 2)),
            pltpu.SemaphoreType.DMA((18, 4, 2)),
        ],
        compiler_params=pltpu.CompilerParams(
            collective_id=0, has_side_effects=True, vmem_limit_bytes=56 * 1024 * 1024
        ),
    )(info, hidden, queries, keys, down, direction, cosine, sine, wT, up)


def reduce_kernel(
    mixed, upT, curv, hidden, direction, up_direction, down_out, up_out, curv_out,
    got_y, sum_y, got_z, part, got_core, sum_core, got_xy, ups, got_uy, sum_dy, got_dz, all_dp,
    send_sem, recv_sem,
):
    z, y = place()
    ctx = lax.axis_index("ctx")
    dp = lax.axis_index("dp")
    x, core = dp // 2, lax.rem(dp, 2)
    barrier = pltpu.get_barrier_semaphore()

    def at_y(o):
        return {"ctx": z * NY + lax.rem(y + o, NY)}

    def at_z(o):
        return {"ctx": lax.rem(z + o, NZ) * NY + y}

    def at_dp(o):
        return {"dp": lax.rem(dp + o, 8)}

    def at_xy(ox, oy):
        return {"dp": lax.rem(x + ox, NX) * 2 + core, "ctx": z * NY + lax.rem(y + oy, NY)}

    plane = [(ox, oy) for ox in range(NX) for oy in range(NY) if ox or oy]
    for ox, oy in plane:
        pl.semaphore_signal(barrier, inc=1, device_id=at_xy(ox, oy), device_id_type=MESH)
    for o in range(1, NZ):
        pl.semaphore_signal(barrier, inc=1, device_id=at_z(o), device_id_type=MESH)
    for o in range(NX):
        other = {"dp": lax.rem(x + o, NX) * 2 + 1 - core}
        pl.semaphore_signal(barrier, inc=1, device_id=other, device_id_type=MESH)

    used = [0]
    sent = []

    def send(src, dst, to):
        copy = pltpu.make_async_remote_copy(
            src_ref=src, dst_ref=dst, send_sem=send_sem.at[used[0]], recv_sem=recv_sem.at[used[0]],
            device_id=to, device_id_type=MESH,
        )
        used[0] += 1
        copy.start()
        sent.append(copy)
        return copy

    pl.semaphore_wait(barrier, 26)

    copies = [
        send(mixed.at[:, lax.rem(y + o, NY)], got_y.at[o - 1], at_y(o)) for o in range(1, NY)
    ]
    for i in range(32):
        block = upT[16 * i : 16 * i + 16, :]
        ups[i % NY, i // NY] = jnp.concatenate([block[0:8], block[8:16]], axis=1)
    for i in range(NY):
        ups[i, NZ] = curv[...]

    def squares(i, acc):
        d = direction[:, pl.ds(pl.multiple_of(i * 512, 512), 512)].astype(F32)
        return acc + jnp.sum((d * d).reshape(8, 8, 512), axis=0)

    squared = jnp.sum(lax.fori_loop(0, 16, squares, jnp.zeros((8, 512), F32)))
    ud = up_direction[...].astype(F32)
    squared = squared + jnp.sum(ud * ud)

    for copy in copies:
        copy.wait_recv()

    def add_y(i, _):
        acc = mixed[i, y].astype(F32)
        for o in range(NY - 1):
            acc = acc + got_y[o, i].astype(F32)
        sum_y[i] = acc.astype(BF)
        return 0

    lax.fori_loop(0, NZ, add_y, 0)
    copies = [
        send(sum_y.at[lax.rem(z + o, NZ)], got_z.at[o - 1], at_z(o)) for o in range(1, NZ)
    ]
    for copy in copies:
        copy.wait_recv()
    own = sum_y[z].astype(F32)
    for o in range(NZ - 1):
        own = own + got_z[o].astype(F32)
    own = own.astype(BF)

    def down(i, _):
        d = dot(own, hidden[:, pl.ds(pl.multiple_of(i * 256, 256), 256)])
        for r in range(8):
            rows = d[8 * r : 8 * r + 8]
            part[r // 2, r % 2, i] = jnp.concatenate([rows[:, 0:HW], rows[:, HW:]], axis=0).astype(BF)
        return 0

    lax.fori_loop(0, 32, down, 0)

    copy = send(part.at[:, 1 - core], got_core, {"dp": x * 2 + 1 - core})
    copy.wait_recv()

    def add_core(i, _):
        for xx in range(NX):
            sum_core[xx, i % NY, i // NY] = (part[xx, core, i].astype(F32) + got_core[xx, i].astype(F32)).astype(BF)
        return 0

    lax.fori_loop(0, 32, add_core, 0)
    copies = []
    for k, (ox, oy) in enumerate(plane):
        copies.append(
            send(sum_core.at[lax.rem(x + ox, NX), lax.rem(y + oy, NY)], got_xy.at[k], at_xy(ox, oy))
        )
    for o in range(1, NY):
        copies.append(send(ups.at[lax.rem(y + o, NY)], got_uy.at[o - 1], at_y(o)))
    for copy in copies:
        copy.wait_recv()
    scal = ups[y, NZ]
    for o in range(NY - 1):
        scal = scal + got_uy[o, NZ]
    for i in range(NZ):
        acc = sum_core[x, y, i].astype(F32)
        for k in range(len(plane)):
            acc = acc + got_xy[k, i].astype(F32)
        upa = ups[y, i]
        for o in range(NY - 1):
            upa = upa + got_uy[o, i]
        sum_dy[i, 0:16] = acc
        sum_dy[i, 16:24] = upa
        sum_dy[i, 24:32] = scal
    copies = [
        send(sum_dy.at[lax.rem(z + o, NZ)], got_dz.at[o - 1], at_z(o)) for o in range(1, NZ)
    ]
    for copy in copies:
        copy.wait_recv()
    acc = sum_dy[z]
    for o in range(NZ - 1):
        acc = acc + got_dz[o]
    all_dp[dp] = acc
    copies = [send(all_dp.at[dp], all_dp.at[dp], at_dp(o)) for o in range(1, 8)]
    for o in range(1, 8):
        slot = lax.rem(dp + 8 - o, 8)
        base = used[0] - 7 + o - 1
        pltpu.make_async_remote_copy(
            src_ref=all_dp.at[slot], dst_ref=all_dp.at[slot], send_sem=send_sem.at[base],
            recv_sem=recv_sem.at[base], device_id=at_dp(o), device_id_type=MESH,
        ).wait_recv()
    tail = all_dp[0, 16:32]
    for r in range(1, 8):
        tail = tail + all_dp[r, 16:32]
    curv_sum = jnp.sum(tail[8:9])
    count = jnp.sum(tail[9:10])
    rescale = squared / (curv_sum + 1e-06)
    for r in range(8):
        down_out[8 * r : 8 * r + 8, 0:HW] = all_dp[r, 0:8] * rescale
        down_out[8 * r : 8 * r + 8, HW : 2 * HW] = all_dp[r, 8:16] * rescale
    up_out[0:8, :] = tail[0:8, 0:RANK] * rescale
    up_out[8:16, :] = tail[0:8, RANK:HW] * rescale
    curv_out[...] = jnp.full((8, HW), curv_sum / count, F32)
    for copy in sent:
        copy.wait_send()


def reduce(mixed, upT, curv, hidden, direction, up_direction):
    return pl.pallas_call(
        reduce_kernel,
        out_shape=(
            jax.ShapeDtypeStruct((RANK, 256), F32),
            jax.ShapeDtypeStruct((16, RANK), F32),
            jax.ShapeDtypeStruct((8, HW), F32),
        ),
        in_specs=[VM] * 6,
        out_specs=(VM, VM, VM),
        scratch_shapes=[
            pltpu.VMEM((NY - 1, NZ, RANK, HW), BF),
            pltpu.VMEM((NZ, RANK, HW), BF),
            pltpu.VMEM((NZ - 1, RANK, HW), BF),
            pltpu.VMEM((NX, 2, 32, 16, HW), BF),
            pltpu.VMEM((NX, 32, 16, HW), BF),
            pltpu.VMEM((NX, NY, NZ, 16, HW), BF),
            pltpu.VMEM((NX * NY - 1, NZ, 16, HW), BF),
            pltpu.VMEM((NY, NZ + 1, 8, HW), F32),
            pltpu.VMEM((NY - 1, NZ + 1, 8, HW), F32),
            pltpu.VMEM((NZ, 32, HW), F32),
            pltpu.VMEM((NZ - 1, 32, HW), F32),
            pltpu.VMEM((8, 32, HW), F32),
            pltpu.SemaphoreType.DMA((43,)),
            pltpu.SemaphoreType.DMA((43,)),
        ],
        compiler_params=pltpu.CompilerParams(
            collective_id=1, has_side_effects=True, vmem_limit_bytes=48 * 1024 * 1024
        ),
    )(mixed, upT, curv, hidden, direction, up_direction)


def body(hidden, queries, keys, down, up, direction, up_direction, window, lengths):
    seq = hidden.shape[1]
    span = seq * NZ * NY
    ctx = lax.axis_index("ctx")
    position = window[0] * span + ctx * seq + jnp.arange(seq, dtype=jnp.int32)
    inv_freq = jnp.exp(jnp.arange(HW // 2, dtype=F32) * (-2.0 * math.log(1000000.0) / HW))
    angles = position.astype(F32)[:, None] * inv_freq
    cosine, sine = jnp.cos(angles), jnp.sin(angles)
    cosine = jnp.concatenate([cosine, cosine], axis=1)
    sine = jnp.concatenate([-sine, sine], axis=1)
    info = (lengths - window * span).astype(jnp.int32)
    wT = jnp.concatenate([up_direction, up], axis=0).T
    mixed, upT, curv = attention(
        info, hidden[0], queries[0], keys[0], down.T, direction.T, cosine, sine, wT, up
    )
    down_out, up_out, curv_out = reduce(mixed, upT, curv, hidden[0], direction.T, up_direction)
    return down_out.T, up_out.T, curv_out[0, 0]


def solution(mesh):
    placed = (
        P("dp", "ctx", None),
        P("dp", "ctx", None),
        P("dp", "ctx", None),
        P(),
        P(),
        P(),
        P(),
        P("dp"),
        P("dp"),
    )
    return jax.shard_map(
        body,
        mesh=mesh,
        in_specs=placed,
        out_specs=(P("ctx", None), P(None, "ctx"), P()),
        check_vma=False,
    )
```

```python
import functools
import math

import jax
import jax.numpy as jnp
from jax import lax
from jax.experimental import pallas as pl
from jax.experimental.pallas import tpu as pltpu
from jax.sharding import PartitionSpec as P

HW = 128
GROUP = 8
RANK = 64
NZ, NY, NX = 8, 4, 4
ROWS = 256
CHUNK = 2048
SUB = 256
F32 = jnp.float32
BF = jnp.bfloat16
MESH = pl.DeviceIdType.MESH
NN = (((1,), (0,)), ((), ()))
NT = (((1,), (1,)), ((), ()))
VM = pl.BlockSpec(memory_space=pltpu.VMEM)
SM = pl.BlockSpec(memory_space=pltpu.SMEM)


def dot(a, b, dims=NN):
    return lax.dot_general(a, b, dims, preferred_element_type=F32)


def place():
    ctx = lax.axis_index("ctx")
    return ctx // NY, lax.rem(ctx, NY)


def forward(size):
    steps = [[(-k, 1, None), (k, -1, None)] for k in range(size // 2 - 1)]
    last = size // 2 - 1
    return steps + [[(-last, 1, 0), (last, -1, 1)]]


DIRECT4 = [[(0, 1, None), (0, -1, None), (0, 2, None)]]
THREE8 = [
    [(0, 1, None), (0, -1, None)],
    [(-1, 1, None), (1, -1, None)],
    [(-2, 1, None), (2, -1, None), (-2, 2, 0), (2, -2, 1)],
]
TWO8 = [
    [(0, 1, None), (0, -1, None), (0, 2, None), (0, -2, None)],
    [(-2, 1, None), (2, -1, None), (-2, 2, 0), (2, -2, 1)],
]


class Flow:
    def __init__(self, index, size, here, plan, block, peer, sems):
        self.index, self.size, self.here, self.plan = index, size, here, plan
        self.block, self.peer = block, peer
        self.send_sem, self.recv_sem = sems
        self.step = -1

    def copy(self, step, k, arriving):
        held, hop, half = self.plan[step][k]
        origin = held - hop if arriving else held
        ref = self.block(lax.rem(self.here + origin + 2 * self.size, self.size), half)
        return pltpu.make_async_remote_copy(
            src_ref=ref,
            dst_ref=ref,
            send_sem=self.send_sem.at[self.index, step, k],
            recv_sem=self.recv_sem.at[self.index, step, k],
            device_id=self.peer(lax.rem(self.here + hop + self.size, self.size)),
            device_id_type=MESH,
        )

    def send(self, step):
        self.step = step
        for k in range(len(self.plan[step])):
            self.copy(step, k, False).start()

    def receive(self, step):
        for k in range(len(self.plan[step])):
            self.copy(step, k, True).wait_recv()
        return sorted({(held - hop) % self.size for held, hop, _ in self.plan[step]})

    def advance(self):
        step = self.step
        came = self.receive(step)
        end = step + 1 == len(self.plan)
        if not end:
            self.send(step + 1)
        return came, end

    def drain(self):
        for step, moves in enumerate(self.plan):
            for k in range(len(moves)):
                self.copy(step, k, False).wait_send()


def cut(ref, half, axis):
    if half is None:
        return ref
    return ref.at[(slice(None),) * axis + (pl.ds(half * 64, 64),)]


def fisher_kernel(
    info, hidden_any, queries_any, keys, down_any, direction_any, up_direction, cosine, sine, wT, up,
    down_out, up_out, curv_out,
    hidden, queries, down, direction, load_sem,
    gath, qT, s_even, s_odd, p_even, p_odd, vT, act, grad, oacc, w_even, w_odd, curv_acc, mixed, upT,
    got_y, sum_y, got_z, part, got_core, sum_core, got_xy, ups, got_uy, sum_dy, got_dz, all_dp,
    gsend, grecv, send_sem, recv_sem,
):
    z, y = place()
    dp = lax.axis_index("dp")
    x, core = dp // 2, lax.rem(dp, 2)
    loads = [
        pltpu.make_async_copy(src, dst, load_sem.at[k])
        for k, (src, dst) in enumerate(
            ((hidden_any, hidden), (down_any, down), (direction_any, direction), (queries_any, queries))
        )
    ]
    for copy in loads:
        copy.start()
    barrier = pltpu.get_barrier_semaphore()

    def at(zz, yy):
        return {"ctx": zz * NY + yy}

    def at_y(o):
        return {"ctx": z * NY + lax.rem(y + o, NY)}

    def at_z(o):
        return {"ctx": lax.rem(z + o, NZ) * NY + y}

    def at_dp(o):
        return {"dp": lax.rem(dp + o, 8)}

    def at_xy(ox, oy):
        return {"dp": lax.rem(x + ox, NX) * 2 + core, "ctx": z * NY + lax.rem(y + oy, NY)}

    plane = [(ox, oy) for ox in range(NX) for oy in range(NY) if ox or oy]
    for ox, oy in plane:
        pl.semaphore_signal(barrier, inc=1, device_id=at_xy(ox, oy), device_id_type=MESH)
    for o in range(1, NZ):
        pl.semaphore_signal(barrier, inc=1, device_id=at_z(o), device_id_type=MESH)
    for o in range(NX):
        other = {"dp": lax.rem(x + o, NX) * 2 + 1 - core}
        pl.semaphore_signal(barrier, inc=1, device_id=other, device_id_type=MESH)

    ys = [lax.rem(y + o, NY) for o in range(NY)]
    zs = [lax.rem(z + o, NZ) for o in range(NZ)]
    cos, sin = cosine[...], sine[...]

    def turn(u):
        u = u.astype(F32)
        return u * cos + pltpu.roll(u, HW // 2, 1) * sin

    for g in range(4):
        gath[1 + g, z, y] = turn(keys[:, g * HW : (g + 1) * HW]).astype(BF)
    for copy in loads[:3]:
        copy.wait()
    gath[0, z, y, 0:RANK, :] = dot(down[...], hidden[...], NT).astype(BF)
    gath[0, z, y, RANK:HW, :] = dot(direction[...], hidden[...], NT).astype(BF)
    pl.semaphore_wait(barrier, 26)

    made = []
    sems = (gsend, grecv)

    def ring_y(plan, block):
        made.append(Flow(len(made), NY, y, plan, block, lambda to: at(z, to), sems))
        return made[-1]

    def ring_z(plan, block):
        made.append(Flow(len(made), NZ, z, plan, block, lambda to: at(to, y), sems))
        return made[-1]

    def y_lane(head, zz, plan):
        return ring_y(plan, lambda o, half: cut(gath.at[head, zz, o], half, 0))

    def z_lane(head, yy, plan):
        return ring_z(plan, lambda o, half: cut(gath.at[head, o, yy], half, 0))

    first_y, first_z = y_lane(0, z, DIRECT4), z_lane(1, y, TWO8)
    act_lanes = {0: z_lane(0, y, forward(NZ))}
    key_lanes = [y_lane(1, z, forward(NY))]
    for flow in (first_z, key_lanes[0], first_y, act_lanes[0]):
        flow.send(0)

    loads[3].wait()
    scale = math.log2(math.e) / math.sqrt(HW)

    def rotate_queries(i, _):
        for h in range(ROWS // HW):
            u = queries[:, pl.ds(pl.multiple_of(i * ROWS + h * HW, HW), HW)]
            qT[i, :, h * HW : (h + 1) * HW] = jnp.transpose(turn(u) * scale).astype(BF)
        return 0

    lax.fori_loop(0, qT.shape[0], rotate_queries, 0)

    kvh = 4
    blocks = NZ * NY
    span = blocks * HW
    per = CHUNK // HW
    me, live = z * NY + y, info[0]
    chunks = me // per + 1
    per_g = GROUP * HW // ROWS
    total = kvh * per_g
    zper = per // NY

    def tangents(zz, yy):
        cols = pl.ds(pl.multiple_of((zz * NY + yy) * HW, HW), HW)
        vv = dot(wT[...], gath[0, zz, yy]).astype(BF)
        for g in range(kvh):
            vT[g, 0:HW, cols] = vv[g * HW : (g + 1) * HW]
        act[:, cols] = gath[0, zz, yy, 0:RANK, :]

    tangents(z, y)
    ones = jnp.where(lax.broadcasted_iota(jnp.int32, (16, span), 0) == 0, 1.0, 0.0).astype(BF)
    for g in range(kvh):
        vT[g, HW : HW + 16, :] = ones
    grad[...] = jnp.zeros_like(grad)
    curv_acc[...] = jnp.zeros_like(curv_acc)

    for slot in range(1, 5):
        new_keys, new_acts, landed = [], {}, []
        if slot <= 2:
            came, _ = first_z.advance()
            new_keys = [y_lane(1, zs[o], forward(NY) if slot == 1 else DIRECT4) for o in came]
        for flow in list(key_lanes):
            if flow.advance()[1]:
                key_lanes.remove(flow)
        for flow in new_keys:
            flow.send(0)
        key_lanes += new_keys
        if slot == 1:
            came, _ = first_y.advance()
            new_acts = {o: z_lane(0, ys[o], THREE8) for o in came}
            landed += [(0, o) for o in came]
        for o, flow in list(act_lanes.items()):
            came, end = flow.advance()
            landed += [(oz, o) for oz in came]
            if end:
                del act_lanes[o]
        for flow in new_acts.values():
            flow.send(0)
        act_lanes.update(new_acts)
        if slot == 2:
            keys2_y = y_lane(2, z, DIRECT4)
            keys2_y.send(0)
            keys34_z = ring_z(THREE8, lambda o, half: cut(gath.at[3:5, o, y], half, 1))
            keys34_z.send(0)
        if slot == 3:
            keys2_y.receive(0)
            keys2_z = ring_z(THREE8, lambda o, half: cut(gath.at[2, o], half, 1))
            keys2_z.send(0)
            keys34_z.advance()
        if slot == 4:
            keys2_z.advance()
            keys34_z.advance()
        for oz, oy in landed:
            tangents(zs[oz], ys[oy])
    assert not key_lanes and not act_lanes

    s_bufs, p_bufs, w_bufs = (s_even, s_odd), (p_even, p_odd), (w_even, w_odd)
    qpos = me * HW + lax.rem(lax.broadcasted_iota(jnp.int32, (1, ROWS), 1), HW)
    liverow = (qpos < live).astype(F32)

    def step(i, even, score, weigh, back, m_prev):
        odd = 1 - even
        if weigh:
            oacc[...] = jnp.zeros_like(oacc)
        q = qT[i] if score else None

        def body(j, mx):
            o = None
            for u in range(CHUNK // SUB):
                us = pl.multiple_of(j * CHUNK + u * SUB, SUB)
                if back:
                    grad[(i - 2) // per_g, :, pl.ds(us, SUB)] += dot(
                        w_bufs[even][...], p_bufs[even][pl.ds(us, SUB), :], NT
                    )
                if score:
                    b = u * (SUB // HW)
                    kc = gath[1 + i // per_g, j * zper + b // NY, b % NY : b % NY + SUB // HW].reshape(SUB, HW)
                    s = dot(kc, q)
                    kpos = us + lax.broadcasted_iota(jnp.int32, (SUB, ROWS), 0)
                    s = jnp.where(kpos <= qpos, s, -1e30)
                    s_bufs[even][pl.ds(us, SUB), :] = s
                    mx = jnp.maximum(mx, jnp.max(s.reshape(SUB // 8, 8, ROWS), axis=0))
                if weigh:
                    p = jnp.exp2(s_bufs[odd][pl.ds(us, SUB), :] - m_prev).astype(BF)
                    p_bufs[odd][pl.ds(us, SUB), :] = p
                    t = dot(vT[(i - 1) // per_g, :, pl.ds(us, SUB)], p)
                    o = t if o is None else o + t
            if weigh:
                oacc[...] += o
            return mx

        mx = lax.fori_loop(0, chunks, body, jnp.full((8, ROWS), -1e30, F32))
        if weigh:
            o = oacc[...]
            inv = 1.0 / o[HW : HW + 1]
            out = o[0:HW] * inv * liverow
            curv_acc[...] += jnp.sum((out * out).reshape(HW // 8, 8, ROWS), axis=0)
            w_bufs[odd][...] = (out * inv).astype(BF)
        return jnp.max(mx, axis=0, keepdims=True)

    def y_rest(head):
        return ring_y(forward(NY), lambda o, half: cut(gath.at[head, :, o], half, 1))

    top = step(0, 0, True, False, False, None)
    keys2_z.advance()
    keys34_z.advance()
    keys3_y, keys4_y = y_rest(3), y_rest(4)
    keys3_y.send(0)
    keys4_y.send(0)
    top = step(1, 1, True, True, False, top)

    def pair(i, top):
        @pl.when(i == 2)
        def _():
            keys2_z.receive(2)
            keys3_y.receive(0)
            keys3_y.send(1)

        @pl.when(i == 3)
        def _():
            keys4_y.receive(0)
            keys4_y.send(1)

        @pl.when(i == 4)
        def _():
            keys3_y.receive(1)

        @pl.when(i == 6)
        def _():
            keys4_y.receive(1)

        top = step(2 * i, 0, True, True, True, top)
        return step(2 * i + 1, 1, True, True, True, top)

    top = lax.fori_loop(1, total // 2, pair, top)
    step(total, 0, False, True, True, top)
    step(total + 1, 1, False, False, True, None)

    used = [0]
    sent = []

    def send(src, dst, to):
        copy = pltpu.make_async_remote_copy(
            src_ref=src, dst_ref=dst, send_sem=send_sem.at[used[0]], recv_sem=recv_sem.at[used[0]],
            device_id=to, device_id_type=MESH,
        )
        used[0] += 1
        copy.start()
        sent.append(copy)
        return copy

    mixed[...] = jnp.zeros_like(mixed)
    upT[...] = jnp.zeros_like(upT)

    def mix(j, _):
        ks = pl.multiple_of(j * CHUNK, CHUNK)
        acc = sum(
            dot(up[:, g * HW : (g + 1) * HW], grad[g, :, pl.ds(ks, CHUNK)].astype(BF)) for g in range(kvh)
        ).astype(BF)
        for b in range(per):
            mixed[j * zper + b // NY, b % NY] = acc[:, b * HW : (b + 1) * HW]
        return 0

    lax.fori_loop(0, chunks, mix, 0)

    copies = [
        send(mixed.at[:, lax.rem(y + o, NY)], got_y.at[o - 1], at_y(o)) for o in range(1, NY)
    ]

    def ascend(j, _):
        ks = pl.multiple_of(j * CHUNK, CHUNK)
        for g in range(kvh):
            upT[g * HW : (g + 1) * HW, :] += dot(
                grad[g, :, pl.ds(ks, CHUNK)].astype(BF), act[:, pl.ds(ks, CHUNK)], NT
            )
        return 0

    lax.fori_loop(0, chunks, ascend, 0)
    both = curv_acc[:, 0:HW] + curv_acc[:, HW : 2 * HW]
    row = lax.broadcasted_iota(jnp.int32, (8, HW), 0)
    lane = lax.broadcasted_iota(jnp.int32, (8, HW), 1)
    mine = ((me * HW + lane) < live).astype(F32)
    curv = jnp.where(
        row == 0, jnp.sum(both, axis=0, keepdims=True), jnp.where(row == 1, mine, 0.0)
    )
    for i in range(32):
        block = upT[16 * i : 16 * i + 16, :]
        ups[i % NY, i // NY] = jnp.concatenate([block[0:8], block[8:16]], axis=1)
    for i in range(NY):
        ups[i, NZ] = curv

    def squares(i, acc):
        d = direction[:, pl.ds(pl.multiple_of(i * 512, 512), 512)].astype(F32)
        return acc + jnp.sum((d * d).reshape(8, 8, 512), axis=0)

    squared = jnp.sum(lax.fori_loop(0, 16, squares, jnp.zeros((8, 512), F32)))
    ud = up_direction[...].astype(F32)
    squared = squared + jnp.sum(ud * ud)

    for copy in copies:
        copy.wait_recv()

    def add_y(i, _):
        acc = mixed[i, y].astype(F32)
        for o in range(NY - 1):
            acc = acc + got_y[o, i].astype(F32)
        sum_y[i] = acc.astype(BF)
        return 0

    lax.fori_loop(0, NZ, add_y, 0)
    copies = [
        send(sum_y.at[lax.rem(z + o, NZ)], got_z.at[o - 1], at_z(o)) for o in range(1, NZ)
    ]
    for copy in copies:
        copy.wait_recv()
    own = sum_y[z].astype(F32)
    for o in range(NZ - 1):
        own = own + got_z[o].astype(F32)
    own = own.astype(BF)

    def make_down(h):
        def down_block(i, _):
            for u in range(2):
                k = 2 * i + u
                d = dot(own, hidden[:, pl.ds(pl.multiple_of((h * 16 + k) * 256, 256), 256)])
                for r in range(8):
                    rows = d[8 * r : 8 * r + 8]
                    part[h, r // 2, r % 2, k] = jnp.concatenate([rows[:, 0:HW], rows[:, HW:]], axis=0).astype(BF)
            return 0

        lax.fori_loop(0, 8, down_block, 0)
        return send(part.at[h, :, 1 - core], got_core.at[h], {"dp": x * 2 + 1 - core})

    def add_core(h):
        def add(i, _):
            for xx in range(NX):
                sum_core[h, xx, i % NY, i // NY] = (
                    part[h, xx, core, i].astype(F32) + got_core[h, xx, i].astype(F32)
                ).astype(BF)
            return 0

        lax.fori_loop(0, 16, add, 0)
        return [
            send(
                sum_core.at[h, lax.rem(x + ox, NX), lax.rem(y + oy, NY)], got_xy.at[h, k], at_xy(ox, oy)
            )
            for k, (ox, oy) in enumerate(plane)
        ]

    cores = [make_down(0), make_down(1)]
    cores[0].wait_recv()
    first = add_core(0)
    up_copies = [send(ups.at[lax.rem(y + o, NY)], got_uy.at[o - 1], at_y(o)) for o in range(1, NY)]
    cores[1].wait_recv()
    second = add_core(1)
    for h, copies in ((0, first), (1, second)):
        for copy in copies:
            copy.wait_recv()
        for i in range(NZ // 2):
            acc = sum_core[h, x, y, i].astype(F32)
            for k in range(len(plane)):
                acc = acc + got_xy[h, k, i].astype(F32)
            sum_dy[h * (NZ // 2) + i, 0:16] = acc
    for copy in up_copies:
        copy.wait_recv()
    scal = ups[y, NZ]
    for o in range(NY - 1):
        scal = scal + got_uy[o, NZ]
    for i in range(NZ):
        upa = ups[y, i]
        for o in range(NY - 1):
            upa = upa + got_uy[o, i]
        sum_dy[i, 16:24] = upa
        sum_dy[i, 24:32] = scal
    copies = [
        send(sum_dy.at[lax.rem(z + o, NZ)], got_dz.at[o - 1], at_z(o)) for o in range(1, NZ)
    ]
    for copy in copies:
        copy.wait_recv()
    acc = sum_dy[z]
    for o in range(NZ - 1):
        acc = acc + got_dz[o]
    all_dp[dp] = acc
    copies = [send(all_dp.at[dp], all_dp.at[dp], at_dp(o)) for o in range(1, 8)]
    for o in range(1, 8):
        slot = lax.rem(dp + 8 - o, 8)
        base = used[0] - 7 + o - 1
        pltpu.make_async_remote_copy(
            src_ref=all_dp.at[slot], dst_ref=all_dp.at[slot], send_sem=send_sem.at[base],
            recv_sem=recv_sem.at[base], device_id=at_dp(o), device_id_type=MESH,
        ).wait_recv()
    tail = all_dp[0, 16:32]
    for r in range(1, 8):
        tail = tail + all_dp[r, 16:32]
    curv_sum = jnp.sum(tail[8:9])
    count = jnp.sum(tail[9:10])
    rescale = squared / (curv_sum + 1e-06)
    for r in range(8):
        down_out[8 * r : 8 * r + 8, 0:HW] = all_dp[r, 0:8] * rescale
        down_out[8 * r : 8 * r + 8, HW : 2 * HW] = all_dp[r, 8:16] * rescale
    up_out[0:8, :] = tail[0:8, 0:RANK] * rescale
    up_out[8:16, :] = tail[0:8, RANK:HW] * rescale
    curv_out[...] = jnp.full((8, HW), curv_sum / count, F32)
    for flow in made:
        flow.drain()
    for copy in sent:
        copy.wait_send()


def fisher(info, hidden, queries, keys, down, direction, up_direction, cosine, sine, wT, up):
    span = NZ * NY * HW
    half = NZ // 2
    anywhere = pl.BlockSpec(memory_space=pl.ANY)
    return pl.pallas_call(
        fisher_kernel,
        out_shape=(
            jax.ShapeDtypeStruct((RANK, 256), F32),
            jax.ShapeDtypeStruct((16, RANK), F32),
            jax.ShapeDtypeStruct((8, HW), F32),
        ),
        in_specs=[SM, anywhere, anywhere, VM, anywhere, anywhere, VM, VM, VM, VM, VM],
        out_specs=(VM, VM, VM),
        scratch_shapes=[
            pltpu.VMEM(hidden.shape, BF),
            pltpu.VMEM(queries.shape, BF),
            pltpu.VMEM(down.shape, BF),
            pltpu.VMEM(direction.shape, BF),
            pltpu.SemaphoreType.DMA((4,)),
            pltpu.VMEM((5, NZ, NY, HW, HW), BF),
            pltpu.VMEM((queries.shape[1] // ROWS, HW, ROWS), BF),
            pltpu.VMEM((span, ROWS), F32),
            pltpu.VMEM((span, ROWS), F32),
            pltpu.VMEM((span, ROWS), BF),
            pltpu.VMEM((span, ROWS), BF),
            pltpu.VMEM((4, HW + 16, span), BF),
            pltpu.VMEM((RANK, span), BF),
            pltpu.VMEM((4, HW, span), F32),
            pltpu.VMEM((HW + 16, ROWS), F32),
            pltpu.VMEM((HW, ROWS), BF),
            pltpu.VMEM((HW, ROWS), BF),
            pltpu.VMEM((8, ROWS), F32),
            pltpu.VMEM((NZ, NY, RANK, HW), BF),
            pltpu.VMEM((4 * HW, RANK), F32),
            pltpu.VMEM((NY - 1, NZ, RANK, HW), BF),
            pltpu.VMEM((NZ, RANK, HW), BF),
            pltpu.VMEM((NZ - 1, RANK, HW), BF),
            pltpu.VMEM((2, NX, 2, 16, 16, HW), BF),
            pltpu.VMEM((2, NX, 16, 16, HW), BF),
            pltpu.VMEM((2, NX, NY, half, 16, HW), BF),
            pltpu.VMEM((2, NX * NY - 1, half, 16, HW), BF),
            pltpu.VMEM((NY, NZ + 1, 8, HW), F32),
            pltpu.VMEM((NY - 1, NZ + 1, 8, HW), F32),
            pltpu.VMEM((NZ, 32, HW), F32),
            pltpu.VMEM((NZ - 1, 32, HW), F32),
            pltpu.VMEM((8, 32, HW), F32),
            pltpu.SemaphoreType.DMA((19, 4, 4)),
            pltpu.SemaphoreType.DMA((19, 4, 4)),
            pltpu.SemaphoreType.DMA((59,)),
            pltpu.SemaphoreType.DMA((59,)),
        ],
        compiler_params=pltpu.CompilerParams(
            collective_id=0, has_side_effects=True, vmem_limit_bytes=58 * 1024 * 1024
        ),
    )(info, hidden, queries, keys, down, direction, up_direction, cosine, sine, wT, up)


def body(hidden, queries, keys, down, up, direction, up_direction, window, lengths):
    seq = hidden.shape[1]
    span = seq * NZ * NY
    ctx = lax.axis_index("ctx")
    position = window[0] * span + ctx * seq + jnp.arange(seq, dtype=jnp.int32)
    inv_freq = jnp.exp(jnp.arange(HW // 2, dtype=F32) * (-2.0 * math.log(1000000.0) / HW))
    angles = position.astype(F32)[:, None] * inv_freq
    cosine, sine = jnp.cos(angles), jnp.sin(angles)
    cosine = jnp.concatenate([cosine, cosine], axis=1)
    sine = jnp.concatenate([-sine, sine], axis=1)
    info = (lengths - window * span).astype(jnp.int32)
    wT = jnp.concatenate([up_direction, up], axis=0).T
    down_out, up_out, curv_out = fisher(
        info, hidden[0], queries[0], keys[0], down.T, direction.T, up_direction, cosine, sine, wT, up
    )
    return down_out.T, up_out.T, curv_out[0, 0]


def solution(mesh):
    placed = (
        P("dp", "ctx", None),
        P("dp", "ctx", None),
        P("dp", "ctx", None),
        P(),
        P(),
        P(),
        P(),
        P("dp"),
        P("dp"),
    )
    return jax.shard_map(
        body,
        mesh=mesh,
        in_specs=placed,
        out_specs=(P("ctx", None), P(None, "ctx"), P()),
        check_vma=False,
    )
```

```python
import functools
import math

import jax
import jax.numpy as jnp
from jax import lax
from jax.experimental import pallas as pl
from jax.experimental.pallas import tpu as pltpu
from jax.sharding import PartitionSpec as P

HW = 128
GROUP = 8
RANK = 64
NZ, NY, NX = 8, 4, 4
ROWS = 256
CHUNK = 2048
SUB = 256
F32 = jnp.float32
BF = jnp.bfloat16
MESH = pl.DeviceIdType.MESH
NN = (((1,), (0,)), ((), ()))
NT = (((1,), (1,)), ((), ()))
VM = pl.BlockSpec(memory_space=pltpu.VMEM)
SM = pl.BlockSpec(memory_space=pltpu.SMEM)


def dot(a, b, dims=NN):
    return lax.dot_general(a, b, dims, preferred_element_type=F32)


def place():
    ctx = lax.axis_index("ctx")
    return ctx // NY, lax.rem(ctx, NY)


def forward(size):
    steps = [[(-k, 1, None), (k, -1, None)] for k in range(size // 2 - 1)]
    last = size // 2 - 1
    return steps + [[(-last, 1, 0), (last, -1, 1)]]


DIRECT4 = [[(0, 1, None), (0, -1, None), (0, 2, None)]]
THREE8 = [
    [(0, 1, None), (0, -1, None)],
    [(-1, 1, None), (1, -1, None)],
    [(-2, 1, None), (2, -1, None), (-2, 2, 0), (2, -2, 1)],
]
TWO8 = [
    [(0, 1, None), (0, -1, None), (0, 2, None), (0, -2, None)],
    [(-2, 1, None), (2, -1, None), (-2, 2, 0), (2, -2, 1)],
]


class Flow:
    def __init__(self, index, size, here, plan, block, peer, sems):
        self.index, self.size, self.here, self.plan = index, size, here, plan
        self.block, self.peer = block, peer
        self.send_sem, self.recv_sem = sems
        self.step = -1

    def copy(self, step, k, arriving):
        held, hop, half = self.plan[step][k]
        origin = held - hop if arriving else held
        ref = self.block(lax.rem(self.here + origin + 2 * self.size, self.size), half)
        return pltpu.make_async_remote_copy(
            src_ref=ref,
            dst_ref=ref,
            send_sem=self.send_sem.at[self.index, step, k],
            recv_sem=self.recv_sem.at[self.index, step, k],
            device_id=self.peer(lax.rem(self.here + hop + self.size, self.size)),
            device_id_type=MESH,
        )

    def send(self, step):
        self.step = step
        for k in range(len(self.plan[step])):
            self.copy(step, k, False).start()

    def receive(self, step):
        for k in range(len(self.plan[step])):
            self.copy(step, k, True).wait_recv()
        return sorted({(held - hop) % self.size for held, hop, _ in self.plan[step]})

    def advance(self):
        step = self.step
        came = self.receive(step)
        end = step + 1 == len(self.plan)
        if not end:
            self.send(step + 1)
        return came, end

    def drain(self):
        for step, moves in enumerate(self.plan):
            for k in range(len(moves)):
                self.copy(step, k, False).wait_send()


def cut(ref, half, axis):
    if half is None:
        return ref
    return ref.at[(slice(None),) * axis + (pl.ds(half * 64, 64),)]


def fisher_kernel(
    info, hidden_any, queries_any, keys, down_any, direction_any, up_direction, cosine, sine, up,
    down_out, tail_out,
    hidden, queries, down, direction, load_sem, wT,
    gath, qT, s_even, s_odd, p_even, p_odd, vT, act, grad, oacc, w_even, w_odd, curv_acc, mixed, upT,
    got_y, sum_y, got_z, part, got_core, sum_core, got_xy, ups, got_uy, sum_dy, got_dz, all_dp,
    gsend, grecv, send_sem, recv_sem,
):
    z, y = place()
    dp = lax.axis_index("dp")
    x, core = dp // 2, lax.rem(dp, 2)
    loads = [
        pltpu.make_async_copy(src, dst, load_sem.at[k])
        for k, (src, dst) in enumerate(
            ((hidden_any, hidden), (down_any, down), (direction_any, direction), (queries_any, queries))
        )
    ]
    for copy in loads:
        copy.start()
    barrier = pltpu.get_barrier_semaphore()

    def at(zz, yy):
        return {"ctx": zz * NY + yy}

    def at_y(o):
        return {"ctx": z * NY + lax.rem(y + o, NY)}

    def at_z(o):
        return {"ctx": lax.rem(z + o, NZ) * NY + y}

    def at_dp(o):
        return {"dp": lax.rem(dp + o, 8)}

    def at_xy(ox, oy):
        return {"dp": lax.rem(x + ox, NX) * 2 + core, "ctx": z * NY + lax.rem(y + oy, NY)}

    plane = [(ox, oy) for ox in range(NX) for oy in range(NY) if ox or oy]
    for ox, oy in plane:
        pl.semaphore_signal(barrier, inc=1, device_id=at_xy(ox, oy), device_id_type=MESH)
    for o in range(1, NZ):
        pl.semaphore_signal(barrier, inc=1, device_id=at_z(o), device_id_type=MESH)
    for o in range(NX):
        other = {"dp": lax.rem(x + o, NX) * 2 + 1 - core}
        pl.semaphore_signal(barrier, inc=1, device_id=other, device_id_type=MESH)

    ys = [lax.rem(y + o, NY) for o in range(NY)]
    zs = [lax.rem(z + o, NZ) for o in range(NZ)]
    cos = jnp.concatenate([cosine[...], cosine[...]], axis=1)
    sin = jnp.concatenate([-sine[...], sine[...]], axis=1)

    def turn(u):
        u = u.astype(F32)
        return u * cos + pltpu.roll(u, HW // 2, 1) * sin

    for g in range(4):
        gath[1 + g, z, y] = turn(keys[:, g * HW : (g + 1) * HW]).astype(BF)
    pl.semaphore_wait(barrier, 26)

    made = []
    sems = (gsend, grecv)

    def ring_y(plan, block):
        made.append(Flow(len(made), NY, y, plan, block, lambda to: at(z, to), sems))
        return made[-1]

    def ring_z(plan, block):
        made.append(Flow(len(made), NZ, z, plan, block, lambda to: at(to, y), sems))
        return made[-1]

    def y_lane(head, zz, plan):
        return ring_y(plan, lambda o, half: cut(gath.at[head, zz, o], half, 0))

    def z_lane(head, yy, plan):
        return ring_z(plan, lambda o, half: cut(gath.at[head, o, yy], half, 0))

    def y_rest(head):
        return ring_y(forward(NY), lambda o, half: cut(gath.at[head, :, o], half, 1))

    first_z = z_lane(1, y, TWO8)
    key_lanes = [y_lane(1, z, forward(NY))]
    for flow in (first_z, key_lanes[0]):
        flow.send(0)
    for copy in loads[:3]:
        copy.wait()
    gath[0, z, y, 0:RANK, :] = dot(down[...], hidden[...], NT).astype(BF)
    gath[0, z, y, RANK:HW, :] = dot(direction[...], hidden[...], NT).astype(BF)
    first_y = y_lane(0, z, DIRECT4)
    act_lanes = {0: z_lane(0, y, forward(NZ))}
    for flow in (first_y, act_lanes[0]):
        flow.send(0)

    loads[3].wait()
    scale = math.log2(math.e) / math.sqrt(HW)

    def rotate_queries(i, _):
        for h in range(ROWS // HW):
            u = queries[:, pl.ds(pl.multiple_of(i * ROWS + h * HW, HW), HW)]
            qT[i, :, h * HW : (h + 1) * HW] = jnp.transpose(turn(u) * scale).astype(BF)
        return 0

    def rotate_some(k):
        lax.fori_loop(4 * k, 4 * k + 4, rotate_queries, 0)

    for g in range(4):
        cols = slice(g * HW, (g + 1) * HW)
        block = jnp.concatenate([up_direction[:, cols], up[:, cols]], axis=0).astype(F32)
        wT[cols, :] = jnp.transpose(block).astype(BF)

    kvh = 4
    blocks = NZ * NY
    span = blocks * HW
    per = CHUNK // HW
    me, live = z * NY + y, info[0]
    chunks = me // per + 1
    per_g = GROUP * HW // ROWS
    total = kvh * per_g
    zper = per // NY

    def tangents(zz, yy):
        cols = pl.ds(pl.multiple_of((zz * NY + yy) * HW, HW), HW)
        vv = dot(wT[...], gath[0, zz, yy]).astype(BF)
        for g in range(kvh):
            vT[g, 0:HW, cols] = vv[g * HW : (g + 1) * HW]
        act[:, cols] = gath[0, zz, yy, 0:RANK, :]

    tangents(z, y)
    ones = jnp.where(lax.broadcasted_iota(jnp.int32, (16, span), 0) == 0, 1.0, 0.0).astype(BF)
    for g in range(kvh):
        vT[g, HW : HW + 16, :] = ones
    grad[...] = jnp.zeros_like(grad)
    curv_acc[...] = jnp.zeros_like(curv_acc)
    rotate_some(0)

    for slot in range(1, 5):
        new_keys, new_acts, landed = [], {}, []
        if slot <= 2:
            came, _ = first_z.advance()
            new_keys = [y_lane(1, zs[o], forward(NY) if slot == 1 else DIRECT4) for o in came]
        for flow in list(key_lanes):
            if flow.advance()[1]:
                key_lanes.remove(flow)
        for flow in new_keys:
            flow.send(0)
        key_lanes += new_keys
        if slot == 1:
            came, _ = first_y.advance()
            new_acts = {o: z_lane(0, ys[o], THREE8) for o in came}
            landed += [(0, o) for o in came]
        for o, flow in list(act_lanes.items()):
            came, end = flow.advance()
            landed += [(oz, o) for oz in came]
            if end:
                del act_lanes[o]
        for flow in new_acts.values():
            flow.send(0)
        act_lanes.update(new_acts)
        if slot == 1:
            keys1_z = z_lane(2, y, TWO8)
            keys1_z.send(0)
        if slot == 2:
            keys1_z.advance()
        if slot == 3:
            keys1_z.advance()
            keys1_y = y_rest(2)
            keys1_y.send(0)
            keys2_y = y_lane(3, z, DIRECT4)
            keys2_y.send(0)
        if slot == 4:
            keys2_y.receive(0)
            keys2_z = ring_z(forward(NZ), lambda o, half: cut(gath.at[3, o], half, 1))
            keys2_z.send(0)
            keys3_z = z_lane(4, y, TWO8)
            keys3_z.send(0)
            keys3_y = y_rest(4)
        if slot < 4:
            rotate_some(slot)
        for oz, oy in landed:
            tangents(zs[oz], ys[oy])
    assert not key_lanes and not act_lanes

    s_bufs, p_bufs, w_bufs = (s_even, s_odd), (p_even, p_odd), (w_even, w_odd)
    qpos = me * HW + lax.rem(lax.broadcasted_iota(jnp.int32, (1, ROWS), 1), HW)
    liverow = (qpos < live).astype(F32)

    def step(i, even, score, weigh, back, m_prev):
        odd = 1 - even
        if weigh:
            oacc[...] = jnp.zeros_like(oacc)
        q = qT[i] if score else None

        def body(j, mx):
            o = None
            for u in range(CHUNK // SUB):
                us = pl.multiple_of(j * CHUNK + u * SUB, SUB)
                if back:
                    grad[(i - 2) // per_g, :, pl.ds(us, SUB)] += dot(
                        w_bufs[even][...], p_bufs[even][pl.ds(us, SUB), :], NT
                    )
                if score:
                    b = u * (SUB // HW)
                    kc = gath[1 + i // per_g, j * zper + b // NY, b % NY : b % NY + SUB // HW].reshape(SUB, HW)
                    s = dot(kc, q)
                    kpos = us + lax.broadcasted_iota(jnp.int32, (SUB, ROWS), 0)
                    s = jnp.where(kpos <= qpos, s, -1e30)
                    s_bufs[even][pl.ds(us, SUB), :] = s
                    mx = jnp.maximum(mx, jnp.max(s.reshape(SUB // 8, 8, ROWS), axis=0))
                if weigh:
                    p = jnp.exp2(s_bufs[odd][pl.ds(us, SUB), :] - m_prev).astype(BF)
                    p_bufs[odd][pl.ds(us, SUB), :] = p
                    t = dot(vT[(i - 1) // per_g, :, pl.ds(us, SUB)], p)
                    o = t if o is None else o + t
            if weigh:
                oacc[...] += o
            return mx

        mx = lax.fori_loop(0, chunks, body, jnp.full((8, ROWS), -1e30, F32))
        if weigh:
            o = oacc[...]
            inv = 1.0 / o[HW : HW + 1]
            out = o[0:HW] * inv * liverow
            curv_acc[...] += jnp.sum((out * out).reshape(HW // 8, 8, ROWS), axis=0)
            w_bufs[odd][...] = (out * inv).astype(BF)
        return jnp.max(mx, axis=0, keepdims=True)

    def pass_on(flow, step, then=None):
        def act():
            flow.receive(step)
            if then is not None:
                then[0].send(then[1])

        return act

    hooks = {
        2: [pass_on(keys1_y, 0, (keys1_y, 1)), pass_on(keys2_z, 0, (keys2_z, 1))],
        3: [pass_on(keys3_z, 0, (keys3_z, 1))],
        4: [pass_on(keys1_y, 1), pass_on(keys2_z, 1, (keys2_z, 2))],
        5: [pass_on(keys3_z, 1, (keys3_y, 0))],
        6: [pass_on(keys2_z, 2, (keys2_z, 3))],
        8: [pass_on(keys2_z, 3)],
        9: [pass_on(keys3_y, 0, (keys3_y, 1))],
        12: [pass_on(keys3_y, 1)],
    }

    def serve(i, odd):
        for n, acts in hooks.items():
            if n % 2 == odd:

                @pl.when(i == n // 2)
                def _():
                    for act in acts:
                        act()

    top = step(0, 0, True, False, False, None)
    top = step(1, 1, True, True, False, top)

    def pair(i, top):
        serve(i, 0)
        top = step(2 * i, 0, True, True, True, top)
        serve(i, 1)
        return step(2 * i + 1, 1, True, True, True, top)

    top = lax.fori_loop(1, total // 2, pair, top)
    step(total, 0, False, True, True, top)
    step(total + 1, 1, False, False, True, None)

    used = [0]
    sent = []

    def send(src, dst, to):
        copy = pltpu.make_async_remote_copy(
            src_ref=src, dst_ref=dst, send_sem=send_sem.at[used[0]], recv_sem=recv_sem.at[used[0]],
            device_id=to, device_id_type=MESH,
        )
        used[0] += 1
        copy.start()
        sent.append(copy)
        return copy

    mixed[...] = jnp.zeros_like(mixed)
    upT[...] = jnp.zeros_like(upT)

    def mix(j, _):
        ks = pl.multiple_of(j * CHUNK, CHUNK)
        acc = sum(
            dot(up[:, g * HW : (g + 1) * HW], grad[g, :, pl.ds(ks, CHUNK)].astype(BF)) for g in range(kvh)
        ).astype(BF)
        for b in range(per):
            mixed[j * zper + b // NY, b % NY] = acc[:, b * HW : (b + 1) * HW]
        return 0

    lax.fori_loop(0, chunks, mix, 0)

    copies = [
        send(mixed.at[:, lax.rem(y + o, NY)], got_y.at[o - 1], at_y(o)) for o in range(1, NY)
    ]

    def ascend(j, _):
        ks = pl.multiple_of(j * CHUNK, CHUNK)
        for g in range(kvh):
            upT[g * HW : (g + 1) * HW, :] += dot(
                grad[g, :, pl.ds(ks, CHUNK)].astype(BF), act[:, pl.ds(ks, CHUNK)], NT
            )
        return 0

    lax.fori_loop(0, chunks, ascend, 0)
    both = curv_acc[:, 0:HW] + curv_acc[:, HW : 2 * HW]
    row = lax.broadcasted_iota(jnp.int32, (8, HW), 0)
    lane = lax.broadcasted_iota(jnp.int32, (8, HW), 1)
    mine = ((me * HW + lane) < live).astype(F32)
    curv = jnp.where(
        row == 0, jnp.sum(both, axis=0, keepdims=True), jnp.where(row == 1, mine, 0.0)
    )
    for i in range(32):
        block = upT[16 * i : 16 * i + 16, :]
        ups[i % NY, i // NY] = jnp.concatenate([block[0:8], block[8:16]], axis=1)
    for i in range(NY):
        ups[i, NZ] = curv

    def squares(i, acc):
        d = direction[:, pl.ds(pl.multiple_of(i * 512, 512), 512)].astype(F32)
        return acc + jnp.sum((d * d).reshape(8, 8, 512), axis=0)

    squared = jnp.sum(lax.fori_loop(0, 16, squares, jnp.zeros((8, 512), F32)))
    ud = up_direction[...].astype(F32)
    squared = squared + jnp.sum(ud * ud)

    for copy in copies:
        copy.wait_recv()

    def add_y(i, _):
        acc = mixed[i, y].astype(F32)
        for o in range(NY - 1):
            acc = acc + got_y[o, i].astype(F32)
        sum_y[i] = acc.astype(BF)
        return 0

    lax.fori_loop(0, NZ, add_y, 0)
    copies = [
        send(sum_y.at[lax.rem(z + o, NZ)], got_z.at[o - 1], at_z(o)) for o in range(1, NZ)
    ]
    for copy in copies:
        copy.wait_recv()
    own = sum_y[z].astype(F32)
    for o in range(NZ - 1):
        own = own + got_z[o].astype(F32)
    own = own.astype(BF)

    def make_down(h):
        def down_block(i, _):
            for u in range(2):
                k = 2 * i + u
                d = dot(own, hidden[:, pl.ds(pl.multiple_of((h * 16 + k) * 256, 256), 256)])
                for r in range(8):
                    rows = d[8 * r : 8 * r + 8]
                    part[h, r // 2, r % 2, k] = jnp.concatenate([rows[:, 0:HW], rows[:, HW:]], axis=0).astype(BF)
            return 0

        lax.fori_loop(0, 8, down_block, 0)
        return send(part.at[h, :, 1 - core], got_core.at[h], {"dp": x * 2 + 1 - core})

    def add_core(h):
        def add(i, _):
            for xx in range(NX):
                sum_core[h, xx, i % NY, i // NY] = (
                    part[h, xx, core, i].astype(F32) + got_core[h, xx, i].astype(F32)
                ).astype(BF)
            return 0

        lax.fori_loop(0, 16, add, 0)
        return [
            send(
                sum_core.at[h, lax.rem(x + ox, NX), lax.rem(y + oy, NY)], got_xy.at[h, k], at_xy(ox, oy)
            )
            for k, (ox, oy) in enumerate(plane)
        ]

    cores = [make_down(0), make_down(1)]
    cores[0].wait_recv()
    first = add_core(0)
    up_copies = [send(ups.at[lax.rem(y + o, NY)], got_uy.at[o - 1], at_y(o)) for o in range(1, NY)]
    cores[1].wait_recv()
    second = add_core(1)
    for h, copies in ((0, first), (1, second)):
        for copy in copies:
            copy.wait_recv()
        for i in range(NZ // 2):
            acc = sum_core[h, x, y, i].astype(F32)
            for k in range(len(plane)):
                acc = acc + got_xy[h, k, i].astype(F32)
            sum_dy[h * (NZ // 2) + i, 0:16] = acc
    for copy in up_copies:
        copy.wait_recv()
    scal = ups[y, NZ]
    for o in range(NY - 1):
        scal = scal + got_uy[o, NZ]
    for i in range(NZ):
        upa = ups[y, i]
        for o in range(NY - 1):
            upa = upa + got_uy[o, i]
        sum_dy[i, 16:24] = upa
        sum_dy[i, 24:32] = scal
    copies = [
        send(sum_dy.at[lax.rem(z + o, NZ)], got_dz.at[o - 1], at_z(o)) for o in range(1, NZ)
    ]
    for copy in copies:
        copy.wait_recv()
    acc = sum_dy[z]
    for o in range(NZ - 1):
        acc = acc + got_dz[o]
    all_dp[dp] = acc
    copies = [send(all_dp.at[dp], all_dp.at[dp], at_dp(o)) for o in range(1, 8)]
    for o in range(1, 8):
        slot = lax.rem(dp + 8 - o, 8)
        base = used[0] - 7 + o - 1
        pltpu.make_async_remote_copy(
            src_ref=all_dp.at[slot], dst_ref=all_dp.at[slot], send_sem=send_sem.at[base],
            recv_sem=recv_sem.at[base], device_id=at_dp(o), device_id_type=MESH,
        ).wait_recv()
    tail = all_dp[0, 16:32]
    for r in range(1, 8):
        tail = tail + all_dp[r, 16:32]
    for r in range(8):
        down_out[8 * r : 8 * r + 8, 0:HW] = all_dp[r, 0:8]
        down_out[8 * r : 8 * r + 8, HW : 2 * HW] = all_dp[r, 8:16]
    tail_out[0:16, :] = tail
    tail_out[16:24, :] = jnp.full((8, HW), squared, F32)
    for flow in made:
        flow.drain()
    for copy in sent:
        copy.wait_send()


def fisher(info, hidden, queries, keys, down, direction, up_direction, cosine, sine, up):
    span = NZ * NY * HW
    half = NZ // 2
    anywhere = pl.BlockSpec(memory_space=pl.ANY)
    return pl.pallas_call(
        fisher_kernel,
        out_shape=(
            jax.ShapeDtypeStruct((RANK, 256), F32),
            jax.ShapeDtypeStruct((24, HW), F32),
        ),
        in_specs=[SM, anywhere, anywhere, VM, anywhere, anywhere, VM, VM, VM, VM],
        out_specs=(VM, VM),
        scratch_shapes=[
            pltpu.VMEM(hidden.shape, BF),
            pltpu.VMEM(queries.shape, BF),
            pltpu.VMEM(down.shape, BF),
            pltpu.VMEM(direction.shape, BF),
            pltpu.SemaphoreType.DMA((4,)),
            pltpu.VMEM((4 * HW, HW), BF),
            pltpu.VMEM((5, NZ, NY, HW, HW), BF),
            pltpu.VMEM((queries.shape[1] // ROWS, HW, ROWS), BF),
            pltpu.VMEM((span, ROWS), F32),
            pltpu.VMEM((span, ROWS), F32),
            pltpu.VMEM((span, ROWS), BF),
            pltpu.VMEM((span, ROWS), BF),
            pltpu.VMEM((4, HW + 16, span), BF),
            pltpu.VMEM((RANK, span), BF),
            pltpu.VMEM((4, HW, span), F32),
            pltpu.VMEM((HW + 16, ROWS), F32),
            pltpu.VMEM((HW, ROWS), BF),
            pltpu.VMEM((HW, ROWS), BF),
            pltpu.VMEM((8, ROWS), F32),
            pltpu.VMEM((NZ, NY, RANK, HW), BF),
            pltpu.VMEM((4 * HW, RANK), F32),
            pltpu.VMEM((NY - 1, NZ, RANK, HW), BF),
            pltpu.VMEM((NZ, RANK, HW), BF),
            pltpu.VMEM((NZ - 1, RANK, HW), BF),
            pltpu.VMEM((2, NX, 2, 16, 16, HW), BF),
            pltpu.VMEM((2, NX, 16, 16, HW), BF),
            pltpu.VMEM((2, NX, NY, half, 16, HW), BF),
            pltpu.VMEM((2, NX * NY - 1, half, 16, HW), BF),
            pltpu.VMEM((NY, NZ + 1, 8, HW), F32),
            pltpu.VMEM((NY - 1, NZ + 1, 8, HW), F32),
            pltpu.VMEM((NZ, 32, HW), F32),
            pltpu.VMEM((NZ - 1, 32, HW), F32),
            pltpu.VMEM((8, 32, HW), F32),
            pltpu.SemaphoreType.DMA((20, 4, 4)),
            pltpu.SemaphoreType.DMA((20, 4, 4)),
            pltpu.SemaphoreType.DMA((59,)),
            pltpu.SemaphoreType.DMA((59,)),
        ],
        compiler_params=pltpu.CompilerParams(
            collective_id=0, has_side_effects=True, vmem_limit_bytes=58 * 1024 * 1024
        ),
    )(info, hidden, queries, keys, down, direction, up_direction, cosine, sine, up)


def scale_kernel(down_sum, tail, down_out, up_out, curv_out):
    curv_sum = jnp.sum(tail[8:9, :])
    count = jnp.sum(tail[9:10, :])
    rescale = tail[16:17, 0:1] / (curv_sum + 1e-06)
    down_out[...] = down_sum[...] * rescale
    up_out[0:8, :] = tail[0:8, 0:RANK] * rescale
    up_out[8:16, :] = tail[0:8, RANK:HW] * rescale
    curv_out[0, 0] = curv_sum / count


def scaled(down_sum, tail):
    return pl.pallas_call(
        scale_kernel,
        out_shape=(
            jax.ShapeDtypeStruct((RANK, 256), F32),
            jax.ShapeDtypeStruct((16, RANK), F32),
            jax.ShapeDtypeStruct((1, 1), F32),
        ),
        in_specs=[VM, VM],
        out_specs=(VM, VM, SM),
    )(down_sum, tail)


def body(hidden, queries, keys, down, up, direction, up_direction, window, lengths):
    seq = hidden.shape[1]
    span = seq * NZ * NY
    ctx = lax.axis_index("ctx")
    position = window[0] * span + ctx * seq + jnp.arange(seq, dtype=jnp.int32)
    inv_freq = jnp.exp(jnp.arange(HW // 2, dtype=F32) * (-2.0 * math.log(1000000.0) / HW))
    angles = position.astype(F32)[:, None] * inv_freq
    cosine, sine = jnp.cos(angles), jnp.sin(angles)
    info = (lengths - window * span).astype(jnp.int32)
    down_sum, tail = fisher(
        info, hidden[0], queries[0], keys[0], down.T, direction.T, up_direction, cosine, sine, up
    )
    down_out, up_out, curv_out = scaled(down_sum, tail)
    return down_out.T, up_out.T, curv_out[0, 0]


def solution(mesh):
    placed = (
        P("dp", "ctx", None),
        P("dp", "ctx", None),
        P("dp", "ctx", None),
        P(),
        P(),
        P(),
        P(),
        P("dp"),
        P("dp"),
    )
    return jax.shard_map(
        body,
        mesh=mesh,
        in_specs=placed,
        out_specs=(P("ctx", None), P(None, "ctx"), P()),
        check_vma=False,
    )
```

```python
import functools
import math

import jax
import jax.numpy as jnp
from jax import lax
from jax.experimental import pallas as pl
from jax.experimental.pallas import tpu as pltpu
from jax.sharding import PartitionSpec as P

HW = 128
GROUP = 8
RANK = 64
NZ, NY, NX = 8, 4, 4
ROWS = 256
CHUNK = 2048
SUB = 256
F32 = jnp.float32
BF = jnp.bfloat16
MESH = pl.DeviceIdType.MESH
NN = (((1,), (0,)), ((), ()))
NT = (((1,), (1,)), ((), ()))
VM = pl.BlockSpec(memory_space=pltpu.VMEM)
SM = pl.BlockSpec(memory_space=pltpu.SMEM)


def dot(a, b, dims=NN):
    return lax.dot_general(a, b, dims, preferred_element_type=F32)


def place():
    ctx = lax.axis_index("ctx")
    return ctx // NY, lax.rem(ctx, NY)


def forward(size):
    steps = [[(-k, 1, None), (k, -1, None)] for k in range(size // 2 - 1)]
    last = size // 2 - 1
    return steps + [[(-last, 1, 0), (last, -1, 1)]]


DIRECT4 = [[(0, 1, None), (0, -1, None), (0, 2, None)]]
THREE8 = [
    [(0, 1, None), (0, -1, None)],
    [(-1, 1, None), (1, -1, None)],
    [(-2, 1, None), (2, -1, None), (-2, 2, 0), (2, -2, 1)],
]
TWO8 = [
    [(0, 1, None), (0, -1, None), (0, 2, None), (0, -2, None)],
    [(-2, 1, None), (2, -1, None), (-2, 2, 0), (2, -2, 1)],
]


class Flow:
    def __init__(self, index, size, here, plan, block, peer, sems):
        self.index, self.size, self.here, self.plan = index, size, here, plan
        self.block, self.peer = block, peer
        self.send_sem, self.recv_sem = sems
        self.step = -1

    def copy(self, step, k, arriving):
        held, hop, half = self.plan[step][k]
        origin = held - hop if arriving else held
        ref = self.block(lax.rem(self.here + origin + 2 * self.size, self.size), half)
        return pltpu.make_async_remote_copy(
            src_ref=ref,
            dst_ref=ref,
            send_sem=self.send_sem.at[self.index, step, k],
            recv_sem=self.recv_sem.at[self.index, step, k],
            device_id=self.peer(lax.rem(self.here + hop + self.size, self.size)),
            device_id_type=MESH,
        )

    def send(self, step):
        self.step = step
        for k in range(len(self.plan[step])):
            self.copy(step, k, False).start()

    def receive(self, step):
        for k in range(len(self.plan[step])):
            self.copy(step, k, True).wait_recv()
        return sorted({(held - hop) % self.size for held, hop, _ in self.plan[step]})

    def advance(self):
        step = self.step
        came = self.receive(step)
        end = step + 1 == len(self.plan)
        if not end:
            self.send(step + 1)
        return came, end

    def drain(self):
        for step, moves in enumerate(self.plan):
            for k in range(len(moves)):
                self.copy(step, k, False).wait_send()


def cut(ref, half, axis):
    if half is None:
        return ref
    return ref.at[(slice(None),) * axis + (pl.ds(half * 64, 64),)]


def fisher_kernel(
    info, hidden_any, queries_any, keys, down_any, direction_any, up_direction, cosine, sine, up,
    down_out, tail_out,
    hidden, queries, down, direction, load_sem, wT,
    gath, qT, s_even, s_odd, p_even, p_odd, vT, act, grad, oacc, w_even, w_odd, curv_acc, mixed, upT,
    got_y, sum_y, got_z, part, got_core, sum_core, got_xy, ups, got_uy, sum_dy, got_dz, all_dp,
    gsend, grecv, send_sem, recv_sem,
):
    z, y = place()
    dp = lax.axis_index("dp")
    x, core = dp // 2, lax.rem(dp, 2)
    loads = [
        pltpu.make_async_copy(src, dst, load_sem.at[k])
        for k, (src, dst) in enumerate(
            ((hidden_any, hidden), (down_any, down), (direction_any, direction), (queries_any, queries))
        )
    ]
    for copy in loads:
        copy.start()
    barrier = pltpu.get_barrier_semaphore()

    def at(zz, yy):
        return {"ctx": zz * NY + yy}

    def at_y(o):
        return {"ctx": z * NY + lax.rem(y + o, NY)}

    def at_z(o):
        return {"ctx": lax.rem(z + o, NZ) * NY + y}

    def at_dp(o):
        return {"dp": lax.rem(dp + o, 8)}

    def at_xy(ox, oy):
        return {"dp": lax.rem(x + ox, NX) * 2 + core, "ctx": z * NY + lax.rem(y + oy, NY)}

    plane = [(ox, oy) for ox in range(NX) for oy in range(NY) if ox or oy]
    for ox, oy in plane:
        pl.semaphore_signal(barrier, inc=1, device_id=at_xy(ox, oy), device_id_type=MESH)
    for o in range(1, NZ):
        pl.semaphore_signal(barrier, inc=1, device_id=at_z(o), device_id_type=MESH)
    for o in range(NX):
        other = {"dp": lax.rem(x + o, NX) * 2 + 1 - core}
        pl.semaphore_signal(barrier, inc=1, device_id=other, device_id_type=MESH)

    ys = [lax.rem(y + o, NY) for o in range(NY)]
    zs = [lax.rem(z + o, NZ) for o in range(NZ)]
    cos = jnp.concatenate([cosine[...], cosine[...]], axis=1)
    sin = jnp.concatenate([-sine[...], sine[...]], axis=1)

    def turn(u):
        u = u.astype(F32)
        return u * cos + pltpu.roll(u, HW // 2, 1) * sin

    for g in range(4):
        gath[1 + g, z, y] = turn(keys[:, g * HW : (g + 1) * HW]).astype(BF)
    pl.semaphore_wait(barrier, 26)

    made = []
    sems = (gsend, grecv)

    def ring_y(plan, block):
        made.append(Flow(len(made), NY, y, plan, block, lambda to: at(z, to), sems))
        return made[-1]

    def ring_z(plan, block):
        made.append(Flow(len(made), NZ, z, plan, block, lambda to: at(to, y), sems))
        return made[-1]

    def y_lane(head, zz, plan):
        return ring_y(plan, lambda o, half: cut(gath.at[head, zz, o], half, 0))

    def z_lane(head, yy, plan):
        return ring_z(plan, lambda o, half: cut(gath.at[head, o, yy], half, 0))

    def y_rest(head):
        return ring_y(forward(NY), lambda o, half: cut(gath.at[head, :, o], half, 1))

    first_z = z_lane(1, y, TWO8)
    key_lanes = [y_lane(1, z, forward(NY))]
    for flow in (first_z, key_lanes[0]):
        flow.send(0)
    for copy in loads[:3]:
        copy.wait()
    gath[0, z, y, 0:RANK, :] = dot(down[...], hidden[...], NT).astype(BF)
    gath[0, z, y, RANK:HW, :] = dot(direction[...], hidden[...], NT).astype(BF)
    first_y = y_lane(0, z, DIRECT4)
    first_y.send(0)

    loads[3].wait()
    scale = math.log2(math.e) / math.sqrt(HW)

    def rotate_queries(i, _):
        for h in range(ROWS // HW):
            u = queries[:, pl.ds(pl.multiple_of(i * ROWS + h * HW, HW), HW)]
            qT[i, :, h * HW : (h + 1) * HW] = jnp.transpose(turn(u) * scale).astype(BF)
        return 0

    def rotate_some(k):
        lax.fori_loop(4 * k, 4 * k + 4, rotate_queries, 0)

    for g in range(4):
        cols = slice(g * HW, (g + 1) * HW)
        block = jnp.concatenate([up_direction[:, cols], up[:, cols]], axis=0).astype(F32)
        wT[cols, :] = jnp.transpose(block).astype(BF)

    kvh = 4
    blocks = NZ * NY
    span = blocks * HW
    per = CHUNK // HW
    me, live = z * NY + y, info[0]
    chunks = me // per + 1
    per_g = GROUP * HW // ROWS
    total = kvh * per_g
    zper = per // NY

    def tangents(zz, yy):
        cols = pl.ds(pl.multiple_of((zz * NY + yy) * HW, HW), HW)
        vv = dot(wT[...], gath[0, zz, yy]).astype(BF)
        for g in range(kvh):
            vT[g, 0:HW, cols] = vv[g * HW : (g + 1) * HW]
        act[:, cols] = gath[0, zz, yy, 0:RANK, :]

    tangents(z, y)
    ones = jnp.where(lax.broadcasted_iota(jnp.int32, (16, span), 0) == 0, 1.0, 0.0).astype(BF)
    for g in range(kvh):
        vT[g, HW : HW + 16, :] = ones
    grad[...] = jnp.zeros_like(grad)
    curv_acc[...] = jnp.zeros_like(curv_acc)
    rotate_some(0)

    s_bufs, p_bufs, w_bufs = (s_even, s_odd), (p_even, p_odd), (w_even, w_odd)
    qpos = me * HW + lax.rem(lax.broadcasted_iota(jnp.int32, (1, ROWS), 1), HW)
    liverow = (qpos < live).astype(F32)

    def step(i, even, score, weigh, back, m_prev):
        odd = 1 - even
        if weigh:
            oacc[...] = jnp.zeros_like(oacc)
        q = qT[i] if score else None

        def body(j, mx):
            o = None
            for u in range(CHUNK // SUB):
                us = pl.multiple_of(j * CHUNK + u * SUB, SUB)
                if back:
                    grad[(i - 2) // per_g, :, pl.ds(us, SUB)] += dot(
                        w_bufs[even][...], p_bufs[even][pl.ds(us, SUB), :], NT
                    )
                if score:
                    b = u * (SUB // HW)
                    kc = gath[1 + i // per_g, j * zper + b // NY, b % NY : b % NY + SUB // HW].reshape(SUB, HW)
                    s = dot(kc, q)
                    kpos = us + lax.broadcasted_iota(jnp.int32, (SUB, ROWS), 0)
                    s = jnp.where(kpos <= qpos, s, -1e30)
                    s_bufs[even][pl.ds(us, SUB), :] = s
                    mx = jnp.maximum(mx, jnp.max(s.reshape(SUB // 8, 8, ROWS), axis=0))
                if weigh:
                    p = jnp.exp2(s_bufs[odd][pl.ds(us, SUB), :] - m_prev).astype(BF)
                    p_bufs[odd][pl.ds(us, SUB), :] = p
                    t = dot(vT[(i - 1) // per_g, :, pl.ds(us, SUB)], p)
                    o = t if o is None else o + t
            if weigh:
                oacc[...] += o
            return mx

        mx = lax.fori_loop(0, chunks, body, jnp.full((8, ROWS), -1e30, F32))
        if weigh:
            o = oacc[...]
            inv = 1.0 / o[HW : HW + 1]
            out = o[0:HW] * inv * liverow
            curv_acc[...] += jnp.sum((out * out).reshape(HW // 8, 8, ROWS), axis=0)
            w_bufs[odd][...] = (out * inv).astype(BF)
        return jnp.max(mx, axis=0, keepdims=True)

    for slot in range(1, 5):
        new_keys, landed = [], []
        if slot <= 2:
            came, _ = first_z.advance()
            new_keys = [y_lane(1, zs[o], forward(NY) if slot == 1 else DIRECT4) for o in came]
        for flow in list(key_lanes):
            if flow.advance()[1]:
                key_lanes.remove(flow)
        for flow in new_keys:
            flow.send(0)
        key_lanes += new_keys
        if slot == 1:
            came, _ = first_y.advance()
            landed += [(0, o) for o in came]
            acts = ring_z(THREE8, lambda o, half: cut(gath.at[0, o], half, 1))
            acts.send(0)
        else:
            came, _ = acts.advance()
            landed += [(oz, oy) for oz in came for oy in range(NY)]
        if slot == 1:
            keys1_z = z_lane(2, y, TWO8)
            keys1_z.send(0)
        if slot == 2:
            keys1_z.advance()
        if slot == 3:
            keys1_z.advance()
            keys1_y = y_rest(2)
            keys1_y.send(0)
            keys2_y = y_lane(3, z, DIRECT4)
            keys2_y.send(0)
        if slot == 4:
            keys2_y.receive(0)
            keys2_z = ring_z(forward(NZ), lambda o, half: cut(gath.at[3, o], half, 1))
            keys2_z.send(0)
            keys3_z = z_lane(4, y, TWO8)
            keys3_z.send(0)
            keys3_y = y_rest(4)
        if slot < 4:
            rotate_some(slot)
        for oz, oy in landed:
            tangents(zs[oz], ys[oy])
        if slot == 3:
            top = step(0, 0, True, False, False, None)

    def pass_on(flow, step, then=None):
        def act():
            flow.receive(step)
            if then is not None:
                then[0].send(then[1])

        return act

    hooks = {
        2: [pass_on(keys1_y, 0, (keys1_y, 1)), pass_on(keys2_z, 0, (keys2_z, 1))],
        3: [pass_on(keys3_z, 0, (keys3_z, 1))],
        4: [pass_on(keys1_y, 1), pass_on(keys2_z, 1, (keys2_z, 2))],
        5: [pass_on(keys3_z, 1, (keys3_y, 0))],
        6: [pass_on(keys2_z, 2, (keys2_z, 3))],
        8: [pass_on(keys2_z, 3)],
        9: [pass_on(keys3_y, 0, (keys3_y, 1))],
        12: [pass_on(keys3_y, 1)],
    }

    def serve(i, odd):
        for n, acts in hooks.items():
            if n % 2 == odd:

                @pl.when(i == n // 2)
                def _():
                    for act in acts:
                        act()

    top = step(1, 1, True, True, False, top)

    def pair(i, top):
        serve(i, 0)
        top = step(2 * i, 0, True, True, True, top)
        serve(i, 1)
        return step(2 * i + 1, 1, True, True, True, top)

    top = lax.fori_loop(1, total // 2, pair, top)
    step(total, 0, False, True, True, top)
    step(total + 1, 1, False, False, True, None)

    used = [0]
    sent = []

    def send(src, dst, to):
        copy = pltpu.make_async_remote_copy(
            src_ref=src, dst_ref=dst, send_sem=send_sem.at[used[0]], recv_sem=recv_sem.at[used[0]],
            device_id=to, device_id_type=MESH,
        )
        used[0] += 1
        copy.start()
        sent.append(copy)
        return copy

    mixed[...] = jnp.zeros_like(mixed)
    upT[...] = jnp.zeros_like(upT)

    def mix(j, _):
        ks = pl.multiple_of(j * CHUNK, CHUNK)
        acc = sum(
            dot(up[:, g * HW : (g + 1) * HW], grad[g, :, pl.ds(ks, CHUNK)].astype(BF)) for g in range(kvh)
        ).astype(BF)
        for b in range(per):
            mixed[j * zper + b // NY, b % NY] = acc[:, b * HW : (b + 1) * HW]
        return 0

    lax.fori_loop(0, chunks, mix, 0)

    copies = [
        send(mixed.at[:, lax.rem(y + o, NY)], got_y.at[o - 1], at_y(o)) for o in range(1, NY)
    ]

    def ascend(j, _):
        ks = pl.multiple_of(j * CHUNK, CHUNK)
        for g in range(kvh):
            upT[g * HW : (g + 1) * HW, :] += dot(
                grad[g, :, pl.ds(ks, CHUNK)].astype(BF), act[:, pl.ds(ks, CHUNK)], NT
            )
        return 0

    lax.fori_loop(0, chunks, ascend, 0)
    both = curv_acc[:, 0:HW] + curv_acc[:, HW : 2 * HW]
    row = lax.broadcasted_iota(jnp.int32, (8, HW), 0)
    lane = lax.broadcasted_iota(jnp.int32, (8, HW), 1)
    mine = ((me * HW + lane) < live).astype(F32)
    curv = jnp.where(
        row == 0, jnp.sum(both, axis=0, keepdims=True), jnp.where(row == 1, mine, 0.0)
    )
    for i in range(32):
        block = upT[16 * i : 16 * i + 16, :]
        ups[i % NY, i // NY] = jnp.concatenate([block[0:8], block[8:16]], axis=1)
    for i in range(NY):
        ups[i, NZ] = curv

    def squares(i, acc):
        d = direction[:, pl.ds(pl.multiple_of(i * 512, 512), 512)].astype(F32)
        return acc + jnp.sum((d * d).reshape(8, 8, 512), axis=0)

    squared = jnp.sum(lax.fori_loop(0, 16, squares, jnp.zeros((8, 512), F32)))
    ud = up_direction[...].astype(F32)
    squared = squared + jnp.sum(ud * ud)

    for copy in copies:
        copy.wait_recv()

    def add_y(i, _):
        acc = mixed[i, y].astype(F32)
        for o in range(NY - 1):
            acc = acc + got_y[o, i].astype(F32)
        sum_y[i] = acc.astype(BF)
        return 0

    lax.fori_loop(0, NZ, add_y, 0)
    copies = [
        send(sum_y.at[lax.rem(z + o, NZ)], got_z.at[o - 1], at_z(o)) for o in range(1, NZ)
    ]
    for copy in copies:
        copy.wait_recv()
    own = sum_y[z].astype(F32)
    for o in range(NZ - 1):
        own = own + got_z[o].astype(F32)
    own = own.astype(BF)

    def make_down(h):
        def down_block(i, _):
            for u in range(2):
                k = 2 * i + u
                d = dot(own, hidden[:, pl.ds(pl.multiple_of((h * 16 + k) * 256, 256), 256)])
                for r in range(8):
                    rows = d[8 * r : 8 * r + 8]
                    part[h, r // 2, r % 2, k] = jnp.concatenate([rows[:, 0:HW], rows[:, HW:]], axis=0).astype(BF)
            return 0

        lax.fori_loop(0, 8, down_block, 0)
        return send(part.at[h, :, 1 - core], got_core.at[h], {"dp": x * 2 + 1 - core})

    def add_core(h):
        def add(i, _):
            for xx in range(NX):
                sum_core[h, xx, i % NY, i // NY] = (
                    part[h, xx, core, i].astype(F32) + got_core[h, xx, i].astype(F32)
                ).astype(BF)
            return 0

        lax.fori_loop(0, 16, add, 0)
        return [
            send(
                sum_core.at[h, lax.rem(x + ox, NX), lax.rem(y + oy, NY)], got_xy.at[h, k], at_xy(ox, oy)
            )
            for k, (ox, oy) in enumerate(plane)
        ]

    cores = [make_down(0), make_down(1)]
    cores[0].wait_recv()
    first = add_core(0)
    up_copies = [send(ups.at[lax.rem(y + o, NY)], got_uy.at[o - 1], at_y(o)) for o in range(1, NY)]
    cores[1].wait_recv()
    second = add_core(1)
    for h, copies in ((0, first), (1, second)):
        for copy in copies:
            copy.wait_recv()
        for i in range(NZ // 2):
            acc = sum_core[h, x, y, i].astype(F32)
            for k in range(len(plane)):
                acc = acc + got_xy[h, k, i].astype(F32)
            sum_dy[h * (NZ // 2) + i, 0:16] = acc
    for copy in up_copies:
        copy.wait_recv()
    scal = ups[y, NZ]
    for o in range(NY - 1):
        scal = scal + got_uy[o, NZ]
    for i in range(NZ):
        upa = ups[y, i]
        for o in range(NY - 1):
            upa = upa + got_uy[o, i]
        sum_dy[i, 16:24] = upa
        sum_dy[i, 24:32] = scal
    copies = [
        send(sum_dy.at[lax.rem(z + o, NZ)], got_dz.at[o - 1], at_z(o)) for o in range(1, NZ)
    ]
    for copy in copies:
        copy.wait_recv()
    acc = sum_dy[z]
    for o in range(NZ - 1):
        acc = acc + got_dz[o]
    all_dp[dp] = acc
    copies = [send(all_dp.at[dp], all_dp.at[dp], at_dp(o)) for o in range(1, 8)]
    for o in range(1, 8):
        slot = lax.rem(dp + 8 - o, 8)
        base = used[0] - 7 + o - 1
        pltpu.make_async_remote_copy(
            src_ref=all_dp.at[slot], dst_ref=all_dp.at[slot], send_sem=send_sem.at[base],
            recv_sem=recv_sem.at[base], device_id=at_dp(o), device_id_type=MESH,
        ).wait_recv()
    tail = all_dp[0, 16:32]
    for r in range(1, 8):
        tail = tail + all_dp[r, 16:32]
    for r in range(8):
        down_out[8 * r : 8 * r + 8, 0:HW] = all_dp[r, 0:8]
        down_out[8 * r : 8 * r + 8, HW : 2 * HW] = all_dp[r, 8:16]
    tail_out[0:16, :] = tail
    tail_out[16:24, :] = jnp.full((8, HW), squared, F32)
    for flow in made:
        flow.drain()
    for copy in sent:
        copy.wait_send()


def fisher(info, hidden, queries, keys, down, direction, up_direction, cosine, sine, up):
    span = NZ * NY * HW
    half = NZ // 2
    anywhere = pl.BlockSpec(memory_space=pl.ANY)
    return pl.pallas_call(
        fisher_kernel,
        out_shape=(
            jax.ShapeDtypeStruct((RANK, 256), F32),
            jax.ShapeDtypeStruct((24, HW), F32),
        ),
        in_specs=[SM, anywhere, anywhere, VM, anywhere, anywhere, VM, VM, VM, VM],
        out_specs=(VM, VM),
        scratch_shapes=[
            pltpu.VMEM(hidden.shape, BF),
            pltpu.VMEM(queries.shape, BF),
            pltpu.VMEM(down.shape, BF),
            pltpu.VMEM(direction.shape, BF),
            pltpu.SemaphoreType.DMA((4,)),
            pltpu.VMEM((4 * HW, HW), BF),
            pltpu.VMEM((5, NZ, NY, HW, HW), BF),
            pltpu.VMEM((queries.shape[1] // ROWS, HW, ROWS), BF),
            pltpu.VMEM((span, ROWS), F32),
            pltpu.VMEM((span, ROWS), F32),
            pltpu.VMEM((span, ROWS), BF),
            pltpu.VMEM((span, ROWS), BF),
            pltpu.VMEM((4, HW + 16, span), BF),
            pltpu.VMEM((RANK, span), BF),
            pltpu.VMEM((4, HW, span), F32),
            pltpu.VMEM((HW + 16, ROWS), F32),
            pltpu.VMEM((HW, ROWS), BF),
            pltpu.VMEM((HW, ROWS), BF),
            pltpu.VMEM((8, ROWS), F32),
            pltpu.VMEM((NZ, NY, RANK, HW), BF),
            pltpu.VMEM((4 * HW, RANK), F32),
            pltpu.VMEM((NY - 1, NZ, RANK, HW), BF),
            pltpu.VMEM((NZ, RANK, HW), BF),
            pltpu.VMEM((NZ - 1, RANK, HW), BF),
            pltpu.VMEM((2, NX, 2, 16, 16, HW), BF),
            pltpu.VMEM((2, NX, 16, 16, HW), BF),
            pltpu.VMEM((2, NX, NY, half, 16, HW), BF),
            pltpu.VMEM((2, NX * NY - 1, half, 16, HW), BF),
            pltpu.VMEM((NY, NZ + 1, 8, HW), F32),
            pltpu.VMEM((NY - 1, NZ + 1, 8, HW), F32),
            pltpu.VMEM((NZ, 32, HW), F32),
            pltpu.VMEM((NZ - 1, 32, HW), F32),
            pltpu.VMEM((8, 32, HW), F32),
            pltpu.SemaphoreType.DMA((17, 4, 4)),
            pltpu.SemaphoreType.DMA((17, 4, 4)),
            pltpu.SemaphoreType.DMA((59,)),
            pltpu.SemaphoreType.DMA((59,)),
        ],
        compiler_params=pltpu.CompilerParams(
            collective_id=0, has_side_effects=True, vmem_limit_bytes=58 * 1024 * 1024
        ),
    )(info, hidden, queries, keys, down, direction, up_direction, cosine, sine, up)


def scale_kernel(down_sum, tail, down_out, up_out, curv_out):
    curv_sum = jnp.sum(tail[8:9, :])
    count = jnp.sum(tail[9:10, :])
    rescale = tail[16:17, 0:1] / (curv_sum + 1e-06)
    down_out[...] = down_sum[...] * rescale
    up_out[0:8, :] = tail[0:8, 0:RANK] * rescale
    up_out[8:16, :] = tail[0:8, RANK:HW] * rescale
    curv_out[0, 0] = curv_sum / count


def scaled(down_sum, tail):
    return pl.pallas_call(
        scale_kernel,
        out_shape=(
            jax.ShapeDtypeStruct((RANK, 256), F32),
            jax.ShapeDtypeStruct((16, RANK), F32),
            jax.ShapeDtypeStruct((1, 1), F32),
        ),
        in_specs=[VM, VM],
        out_specs=(VM, VM, SM),
    )(down_sum, tail)


def body(hidden, queries, keys, down, up, direction, up_direction, window, lengths):
    seq = hidden.shape[1]
    span = seq * NZ * NY
    ctx = lax.axis_index("ctx")
    position = window[0] * span + ctx * seq + jnp.arange(seq, dtype=jnp.int32)
    inv_freq = jnp.exp(jnp.arange(HW // 2, dtype=F32) * (-2.0 * math.log(1000000.0) / HW))
    angles = position.astype(F32)[:, None] * inv_freq
    cosine, sine = jnp.cos(angles), jnp.sin(angles)
    info = (lengths - window * span).astype(jnp.int32)
    down_sum, tail = fisher(
        info, hidden[0], queries[0], keys[0], down.T, direction.T, up_direction, cosine, sine, up
    )
    down_out, up_out, curv_out = scaled(down_sum, tail)
    return down_out.T, up_out.T, curv_out[0, 0]


def solution(mesh):
    placed = (
        P("dp", "ctx", None),
        P("dp", "ctx", None),
        P("dp", "ctx", None),
        P(),
        P(),
        P(),
        P(),
        P("dp"),
        P("dp"),
    )
    return jax.shard_map(
        body,
        mesh=mesh,
        in_specs=placed,
        out_specs=(P("ctx", None), P(None, "ctx"), P()),
        check_vma=False,
    )
```

```python
import functools
import math

import jax
import jax.numpy as jnp
from jax import lax
from jax.experimental import pallas as pl
from jax.experimental.pallas import tpu as pltpu
from jax.sharding import PartitionSpec as P

HW = 128
GROUP = 8
RANK = 64
NZ, NY, NX = 8, 4, 4
ROWS = 256
CHUNK = 2048
SUB = 256
F32 = jnp.float32
BF = jnp.bfloat16
MESH = pl.DeviceIdType.MESH
NN = (((1,), (0,)), ((), ()))
NT = (((1,), (1,)), ((), ()))
VM = pl.BlockSpec(memory_space=pltpu.VMEM)
SM = pl.BlockSpec(memory_space=pltpu.SMEM)


def dot(a, b, dims=NN):
    return lax.dot_general(a, b, dims, preferred_element_type=F32)


def place():
    ctx = lax.axis_index("ctx")
    return ctx // NY, lax.rem(ctx, NY)


def forward(size):
    steps = [[(-k, 1, None), (k, -1, None)] for k in range(size // 2 - 1)]
    last = size // 2 - 1
    return steps + [[(-last, 1, 0), (last, -1, 1)]]


DIRECT4 = [[(0, 1, None), (0, -1, None), (0, 2, None)]]
THREE8 = [
    [(0, 1, None), (0, -1, None)],
    [(-1, 1, None), (1, -1, None)],
    [(-2, 1, None), (2, -1, None), (-2, 2, 0), (2, -2, 1)],
]
TWO8 = [
    [(0, 1, None), (0, -1, None), (0, 2, None), (0, -2, None)],
    [(-2, 1, None), (2, -1, None), (-2, 2, 0), (2, -2, 1)],
]


class Flow:
    def __init__(self, index, size, here, plan, block, peer, sems):
        self.index, self.size, self.here, self.plan = index, size, here, plan
        self.block, self.peer = block, peer
        self.send_sem, self.recv_sem = sems
        self.step = -1

    def copy(self, step, k, arriving):
        held, hop, half = self.plan[step][k]
        origin = held - hop if arriving else held
        ref = self.block(lax.rem(self.here + origin + 2 * self.size, self.size), half)
        return pltpu.make_async_remote_copy(
            src_ref=ref,
            dst_ref=ref,
            send_sem=self.send_sem.at[self.index, step, k],
            recv_sem=self.recv_sem.at[self.index, step, k],
            device_id=self.peer(lax.rem(self.here + hop + self.size, self.size)),
            device_id_type=MESH,
        )

    def send(self, step):
        self.step = step
        for k in range(len(self.plan[step])):
            self.copy(step, k, False).start()

    def receive(self, step):
        for k in range(len(self.plan[step])):
            self.copy(step, k, True).wait_recv()
        return sorted({(held - hop) % self.size for held, hop, _ in self.plan[step]})

    def advance(self):
        step = self.step
        came = self.receive(step)
        end = step + 1 == len(self.plan)
        if not end:
            self.send(step + 1)
        return came, end

    def drain(self):
        for step, moves in enumerate(self.plan):
            for k in range(len(moves)):
                self.copy(step, k, False).wait_send()


def cut(ref, half, axis, rows=64):
    if half is None:
        return ref
    return ref.at[(slice(None),) * axis + (pl.ds(half * rows, rows),)]


def fisher_kernel(
    info, hidden_any, queries_any, keys, down_any, direction_any, up_direction, cosine, sine, up,
    down_out, tail_out,
    hidden, queries, down, direction, load_sem, wT, ranks,
    gath, qT, s_even, s_odd, p_even, p_odd, vT, act, grad, oacc, w_even, w_odd, curv_acc, mixed, upT,
    got_y, sum_y, got_z, part, got_core, sum_core, got_xy, ups, got_uy, sum_dy, got_dz, all_dp,
    gsend, grecv, send_sem, recv_sem,
):
    z, y = place()
    dp = lax.axis_index("dp")
    x, core = dp // 2, lax.rem(dp, 2)
    loads = [
        pltpu.make_async_copy(src, dst, load_sem.at[k])
        for k, (src, dst) in enumerate(
            ((hidden_any, hidden), (down_any, down), (direction_any, direction), (queries_any, queries))
        )
    ]
    for copy in loads:
        copy.start()
    barrier = pltpu.get_barrier_semaphore()

    def at(zz, yy):
        return {"ctx": zz * NY + yy}

    def at_y(o):
        return {"ctx": z * NY + lax.rem(y + o, NY)}

    def at_z(o):
        return {"ctx": lax.rem(z + o, NZ) * NY + y}

    def at_dp(o):
        return {"dp": lax.rem(dp + o, 8)}

    def at_xy(ox, oy):
        return {"dp": lax.rem(x + ox, NX) * 2 + core, "ctx": z * NY + lax.rem(y + oy, NY)}

    plane = [(ox, oy) for ox in range(NX) for oy in range(NY) if ox or oy]
    for ox, oy in plane:
        pl.semaphore_signal(barrier, inc=1, device_id=at_xy(ox, oy), device_id_type=MESH)
    for o in range(1, NZ):
        pl.semaphore_signal(barrier, inc=1, device_id=at_z(o), device_id_type=MESH)
    for o in range(NX):
        other = {"dp": lax.rem(x + o, NX) * 2 + 1 - core}
        pl.semaphore_signal(barrier, inc=1, device_id=other, device_id_type=MESH)

    ys = [lax.rem(y + o, NY) for o in range(NY)]
    zs = [lax.rem(z + o, NZ) for o in range(NZ)]
    cos = jnp.concatenate([cosine[...], cosine[...]], axis=1)
    sin = jnp.concatenate([-sine[...], sine[...]], axis=1)

    def turn(u):
        u = u.astype(F32)
        return u * cos + pltpu.roll(u, HW // 2, 1) * sin

    for g in range(4):
        gath[g, z, y] = turn(keys[:, g * HW : (g + 1) * HW]).astype(BF)
    pl.semaphore_wait(barrier, 26)

    made = []
    sems = (gsend, grecv)

    def ring_y(plan, block):
        made.append(Flow(len(made), NY, y, plan, block, lambda to: at(z, to), sems))
        return made[-1]

    def ring_z(plan, block):
        made.append(Flow(len(made), NZ, z, plan, block, lambda to: at(to, y), sems))
        return made[-1]

    def y_lane(head, zz, plan):
        return ring_y(plan, lambda o, half: cut(gath.at[head, zz, o], half, 0))

    def z_lane(head, yy, plan):
        return ring_z(plan, lambda o, half: cut(gath.at[head, o, yy], half, 0))

    def y_rest(head):
        return ring_y(forward(NY), lambda o, half: cut(gath.at[head, :, o], half, 1))

    first_z = z_lane(0, y, TWO8)
    key_lanes = [y_lane(0, z, forward(NY))]
    for flow in (first_z, key_lanes[0]):
        flow.send(0)
    for copy in loads[:3]:
        copy.wait()
    ranks[0, z, y] = dot(down[...], hidden[...], NT).astype(BF)
    ranks[1, z, y] = dot(direction[...], hidden[...], NT).astype(BF)
    first_y = ring_y(DIRECT4, lambda o, half: ranks.at[0, z, o])
    tans_z = ring_z(TWO8, lambda o, half: cut(ranks.at[1, o, y], half, 0, 32))
    for flow in (first_y, tans_z):
        flow.send(0)

    loads[3].wait()
    scale = math.log2(math.e) / math.sqrt(HW)

    def rotate_queries(i, _):
        for h in range(ROWS // HW):
            u = queries[:, pl.ds(pl.multiple_of(i * ROWS + h * HW, HW), HW)]
            qT[i, :, h * HW : (h + 1) * HW] = jnp.transpose(turn(u) * scale).astype(BF)
        return 0

    def rotate_some(k):
        lax.fori_loop(4 * k, 4 * k + 4, rotate_queries, 0)

    for g in range(4):
        cols = slice(g * HW, (g + 1) * HW)
        block = jnp.concatenate([up_direction[:, cols], up[:, cols]], axis=0).astype(F32)
        wT[cols, :] = jnp.transpose(block).astype(BF)

    kvh = 4
    blocks = NZ * NY
    span = blocks * HW
    per = CHUNK // HW
    me, live = z * NY + y, info[0]
    chunks = me // per + 1
    per_g = GROUP * HW // ROWS
    total = kvh * per_g
    zper = per // NY

    def tangents(zz, yy):
        cols = pl.ds(pl.multiple_of((zz * NY + yy) * HW, HW), HW)
        block = jnp.concatenate([ranks[0, zz, yy], ranks[1, zz, yy]], axis=0)
        vv = dot(wT[...], block).astype(BF)
        for g in range(kvh):
            vT[g, 0:HW, cols] = vv[g * HW : (g + 1) * HW]
        act[:, cols] = ranks[0, zz, yy]

    ones = jnp.where(lax.broadcasted_iota(jnp.int32, (16, span), 0) == 0, 1.0, 0.0).astype(BF)
    for g in range(kvh):
        vT[g, HW : HW + 16, :] = ones
    grad[...] = jnp.zeros_like(grad)
    curv_acc[...] = jnp.zeros_like(curv_acc)
    rotate_some(0)

    s_bufs, p_bufs, w_bufs = (s_even, s_odd), (p_even, p_odd), (w_even, w_odd)
    qpos = me * HW + lax.rem(lax.broadcasted_iota(jnp.int32, (1, ROWS), 1), HW)
    liverow = (qpos < live).astype(F32)

    def step(i, even, score, weigh, back, m_prev):
        odd = 1 - even
        if weigh:
            oacc[...] = jnp.zeros_like(oacc)
        q = qT[i] if score else None

        def body(j, mx):
            o = None
            for u in range(CHUNK // SUB):
                us = pl.multiple_of(j * CHUNK + u * SUB, SUB)
                if back:
                    grad[(i - 2) // per_g, :, pl.ds(us, SUB)] += dot(
                        w_bufs[even][...], p_bufs[even][pl.ds(us, SUB), :], NT
                    )
                if score:
                    b = u * (SUB // HW)
                    kc = gath[i // per_g, j * zper + b // NY, b % NY : b % NY + SUB // HW].reshape(SUB, HW)
                    s = dot(kc, q)
                    kpos = us + lax.broadcasted_iota(jnp.int32, (SUB, ROWS), 0)
                    s = jnp.where(kpos <= qpos, s, -1e30)
                    s_bufs[even][pl.ds(us, SUB), :] = s
                    mx = jnp.maximum(mx, jnp.max(s.reshape(SUB // 8, 8, ROWS), axis=0))
                if weigh:
                    p = jnp.exp2(s_bufs[odd][pl.ds(us, SUB), :] - m_prev).astype(BF)
                    p_bufs[odd][pl.ds(us, SUB), :] = p
                    t = dot(vT[(i - 1) // per_g, :, pl.ds(us, SUB)], p)
                    o = t if o is None else o + t
            if weigh:
                oacc[...] += o
            return mx

        mx = lax.fori_loop(0, chunks, body, jnp.full((8, ROWS), -1e30, F32))
        if weigh:
            o = oacc[...]
            inv = 1.0 / o[HW : HW + 1]
            out = o[0:HW] * inv * liverow
            curv_acc[...] += jnp.sum((out * out).reshape(HW // 8, 8, ROWS), axis=0)
            w_bufs[odd][...] = (out * inv).astype(BF)
        return jnp.max(mx, axis=0, keepdims=True)

    for slot in range(1, 5):
        new_keys = []
        if slot <= 2:
            came, _ = first_z.advance()
            new_keys = [y_lane(0, zs[o], forward(NY) if slot == 1 else DIRECT4) for o in came]
        for flow in list(key_lanes):
            if flow.advance()[1]:
                key_lanes.remove(flow)
        for flow in new_keys:
            flow.send(0)
        key_lanes += new_keys
        if slot == 1:
            first_y.advance()
            acts = ring_z(THREE8, lambda o, half: cut(ranks.at[0, o], half, 1, 32))
            acts.send(0)
            tans_z.advance()
        else:
            acts.advance()
        if slot == 2:
            tans_z.advance()
            tans_y = ring_y(DIRECT4, lambda o, half: ranks.at[1, :, o])
            tans_y.send(0)
        if slot == 3:
            tans_y.advance()
        acts_by = (1, 2, 3, 4, 4, 4, 3, 2)
        tans_by = (2, 3, 3, 3)
        landed = [
            (oz, oy) for oz in range(NZ) for oy in range(NY) if max(acts_by[oz], tans_by[oy]) == slot
        ]
        if slot == 1:
            keys1_z = z_lane(1, y, TWO8)
            keys1_z.send(0)
        if slot == 2:
            keys1_z.advance()
        if slot == 3:
            keys1_z.advance()
            keys1_y = y_rest(1)
            keys1_y.send(0)
            keys2_y = y_lane(2, z, DIRECT4)
            keys2_y.send(0)
        if slot == 4:
            keys2_y.receive(0)
            keys2_z = ring_z(forward(NZ), lambda o, half: cut(gath.at[2, o], half, 1))
            keys2_z.send(0)
            keys3_z = z_lane(3, y, TWO8)
            keys3_z.send(0)
            keys3_y = y_rest(3)
        if slot < 4:
            rotate_some(slot)
        for oz, oy in landed:
            tangents(zs[oz], ys[oy])
        if slot == 3:
            top = step(0, 0, True, False, False, None)

    def pass_on(flow, step, then=None):
        def act():
            flow.receive(step)
            if then is not None:
                then[0].send(then[1])

        return act

    hooks = {
        2: [pass_on(keys1_y, 0, (keys1_y, 1)), pass_on(keys2_z, 0, (keys2_z, 1))],
        3: [pass_on(keys3_z, 0, (keys3_z, 1))],
        4: [pass_on(keys1_y, 1), pass_on(keys2_z, 1, (keys2_z, 2))],
        5: [pass_on(keys3_z, 1, (keys3_y, 0))],
        6: [pass_on(keys2_z, 2, (keys2_z, 3))],
        8: [pass_on(keys2_z, 3)],
        9: [pass_on(keys3_y, 0, (keys3_y, 1))],
        12: [pass_on(keys3_y, 1)],
    }

    def serve(i, odd):
        for n, acts in hooks.items():
            if n % 2 == odd:

                @pl.when(i == n // 2)
                def _():
                    for act in acts:
                        act()

    top = step(1, 1, True, True, False, top)

    def pair(i, top):
        serve(i, 0)
        top = step(2 * i, 0, True, True, True, top)
        serve(i, 1)
        return step(2 * i + 1, 1, True, True, True, top)

    top = lax.fori_loop(1, total // 2, pair, top)
    step(total, 0, False, True, True, top)
    step(total + 1, 1, False, False, True, None)

    used = [0]
    sent = []

    def send(src, dst, to):
        copy = pltpu.make_async_remote_copy(
            src_ref=src, dst_ref=dst, send_sem=send_sem.at[used[0]], recv_sem=recv_sem.at[used[0]],
            device_id=to, device_id_type=MESH,
        )
        used[0] += 1
        copy.start()
        sent.append(copy)
        return copy

    mixed[...] = jnp.zeros_like(mixed)
    upT[...] = jnp.zeros_like(upT)

    def mix(j, _):
        ks = pl.multiple_of(j * CHUNK, CHUNK)
        acc = sum(
            dot(up[:, g * HW : (g + 1) * HW], grad[g, :, pl.ds(ks, CHUNK)].astype(BF)) for g in range(kvh)
        ).astype(BF)
        for b in range(per):
            mixed[j * zper + b // NY, b % NY] = acc[:, b * HW : (b + 1) * HW]
        return 0

    lax.fori_loop(0, chunks, mix, 0)

    copies = [
        send(mixed.at[:, lax.rem(y + o, NY)], got_y.at[o - 1], at_y(o)) for o in range(1, NY)
    ]

    def ascend(j, _):
        ks = pl.multiple_of(j * CHUNK, CHUNK)
        for g in range(kvh):
            upT[g * HW : (g + 1) * HW, :] += dot(
                grad[g, :, pl.ds(ks, CHUNK)].astype(BF), act[:, pl.ds(ks, CHUNK)], NT
            )
        return 0

    lax.fori_loop(0, chunks, ascend, 0)
    both = curv_acc[:, 0:HW] + curv_acc[:, HW : 2 * HW]
    row = lax.broadcasted_iota(jnp.int32, (8, HW), 0)
    lane = lax.broadcasted_iota(jnp.int32, (8, HW), 1)
    mine = ((me * HW + lane) < live).astype(F32)
    curv = jnp.where(
        row == 0, jnp.sum(both, axis=0, keepdims=True), jnp.where(row == 1, mine, 0.0)
    )
    for i in range(32):
        block = upT[16 * i : 16 * i + 16, :]
        ups[i % NY, i // NY] = jnp.concatenate([block[0:8], block[8:16]], axis=1)
    for i in range(NY):
        ups[i, NZ] = curv

    def squares(i, acc):
        d = direction[:, pl.ds(pl.multiple_of(i * 512, 512), 512)].astype(F32)
        return acc + jnp.sum((d * d).reshape(8, 8, 512), axis=0)

    squared = jnp.sum(lax.fori_loop(0, 16, squares, jnp.zeros((8, 512), F32)))
    ud = up_direction[...].astype(F32)
    squared = squared + jnp.sum(ud * ud)

    for copy in copies:
        copy.wait_recv()

    def add_y(i, _):
        acc = mixed[i, y].astype(F32)
        for o in range(NY - 1):
            acc = acc + got_y[o, i].astype(F32)
        sum_y[i] = acc.astype(BF)
        return 0

    lax.fori_loop(0, NZ, add_y, 0)
    copies = [
        send(sum_y.at[lax.rem(z + o, NZ)], got_z.at[o - 1], at_z(o)) for o in range(1, NZ)
    ]
    for copy in copies:
        copy.wait_recv()
    own = sum_y[z].astype(F32)
    for o in range(NZ - 1):
        own = own + got_z[o].astype(F32)
    own = own.astype(BF)

    def make_down(h):
        def down_block(i, _):
            for u in range(2):
                k = 2 * i + u
                d = dot(own, hidden[:, pl.ds(pl.multiple_of((h * 16 + k) * 256, 256), 256)])
                for r in range(8):
                    rows = d[8 * r : 8 * r + 8]
                    part[h, r // 2, r % 2, k] = jnp.concatenate([rows[:, 0:HW], rows[:, HW:]], axis=0).astype(BF)
            return 0

        lax.fori_loop(0, 8, down_block, 0)
        return send(part.at[h, :, 1 - core], got_core.at[h], {"dp": x * 2 + 1 - core})

    def add_core(h):
        def add(i, _):
            for xx in range(NX):
                sum_core[h, xx, i % NY, i // NY] = (
                    part[h, xx, core, i].astype(F32) + got_core[h, xx, i].astype(F32)
                ).astype(BF)
            return 0

        lax.fori_loop(0, 16, add, 0)
        return [
            send(
                sum_core.at[h, lax.rem(x + ox, NX), lax.rem(y + oy, NY)], got_xy.at[h, k], at_xy(ox, oy)
            )
            for k, (ox, oy) in enumerate(plane)
        ]

    cores = [make_down(0), make_down(1)]
    cores[0].wait_recv()
    first = add_core(0)
    up_copies = [send(ups.at[lax.rem(y + o, NY)], got_uy.at[o - 1], at_y(o)) for o in range(1, NY)]
    cores[1].wait_recv()
    second = add_core(1)
    for h, copies in ((0, first), (1, second)):
        for copy in copies:
            copy.wait_recv()
        for i in range(NZ // 2):
            acc = sum_core[h, x, y, i].astype(F32)
            for k in range(len(plane)):
                acc = acc + got_xy[h, k, i].astype(F32)
            sum_dy[h * (NZ // 2) + i, 0:16] = acc
    for copy in up_copies:
        copy.wait_recv()
    scal = ups[y, NZ]
    for o in range(NY - 1):
        scal = scal + got_uy[o, NZ]
    for i in range(NZ):
        upa = ups[y, i]
        for o in range(NY - 1):
            upa = upa + got_uy[o, i]
        sum_dy[i, 16:24] = upa
        sum_dy[i, 24:32] = scal
    copies = [
        send(sum_dy.at[lax.rem(z + o, NZ)], got_dz.at[o - 1], at_z(o)) for o in range(1, NZ)
    ]
    for copy in copies:
        copy.wait_recv()
    acc = sum_dy[z]
    for o in range(NZ - 1):
        acc = acc + got_dz[o]
    all_dp[dp] = acc
    copies = [send(all_dp.at[dp], all_dp.at[dp], at_dp(o)) for o in range(1, 8)]
    for o in range(1, 8):
        slot = lax.rem(dp + 8 - o, 8)
        base = used[0] - 7 + o - 1
        pltpu.make_async_remote_copy(
            src_ref=all_dp.at[slot], dst_ref=all_dp.at[slot], send_sem=send_sem.at[base],
            recv_sem=recv_sem.at[base], device_id=at_dp(o), device_id_type=MESH,
        ).wait_recv()
    tail = all_dp[0, 16:32]
    for r in range(1, 8):
        tail = tail + all_dp[r, 16:32]
    for r in range(8):
        down_out[8 * r : 8 * r + 8, 0:HW] = all_dp[r, 0:8]
        down_out[8 * r : 8 * r + 8, HW : 2 * HW] = all_dp[r, 8:16]
    tail_out[0:16, :] = tail
    tail_out[16:24, :] = jnp.full((8, HW), squared, F32)
    for flow in made:
        flow.drain()
    for copy in sent:
        copy.wait_send()


def fisher(info, hidden, queries, keys, down, direction, up_direction, cosine, sine, up):
    span = NZ * NY * HW
    half = NZ // 2
    anywhere = pl.BlockSpec(memory_space=pl.ANY)
    return pl.pallas_call(
        fisher_kernel,
        out_shape=(
            jax.ShapeDtypeStruct((RANK, 256), F32),
            jax.ShapeDtypeStruct((24, HW), F32),
        ),
        in_specs=[SM, anywhere, anywhere, VM, anywhere, anywhere, VM, VM, VM, VM],
        out_specs=(VM, VM),
        scratch_shapes=[
            pltpu.VMEM(hidden.shape, BF),
            pltpu.VMEM(queries.shape, BF),
            pltpu.VMEM(down.shape, BF),
            pltpu.VMEM(direction.shape, BF),
            pltpu.SemaphoreType.DMA((4,)),
            pltpu.VMEM((4 * HW, HW), BF),
            pltpu.VMEM((2, NZ, NY, RANK, HW), BF),
            pltpu.VMEM((4, NZ, NY, HW, HW), BF),
            pltpu.VMEM((queries.shape[1] // ROWS, HW, ROWS), BF),
            pltpu.VMEM((span, ROWS), F32),
            pltpu.VMEM((span, ROWS), F32),
            pltpu.VMEM((span, ROWS), BF),
            pltpu.VMEM((span, ROWS), BF),
            pltpu.VMEM((4, HW + 16, span), BF),
            pltpu.VMEM((RANK, span), BF),
            pltpu.VMEM((4, HW, span), F32),
            pltpu.VMEM((HW + 16, ROWS), F32),
            pltpu.VMEM((HW, ROWS), BF),
            pltpu.VMEM((HW, ROWS), BF),
            pltpu.VMEM((8, ROWS), F32),
            pltpu.VMEM((NZ, NY, RANK, HW), BF),
            pltpu.VMEM((4 * HW, RANK), F32),
            pltpu.VMEM((NY - 1, NZ, RANK, HW), BF),
            pltpu.VMEM((NZ, RANK, HW), BF),
            pltpu.VMEM((NZ - 1, RANK, HW), BF),
            pltpu.VMEM((2, NX, 2, 16, 16, HW), BF),
            pltpu.VMEM((2, NX, 16, 16, HW), BF),
            pltpu.VMEM((2, NX, NY, half, 16, HW), BF),
            pltpu.VMEM((2, NX * NY - 1, half, 16, HW), BF),
            pltpu.VMEM((NY, NZ + 1, 8, HW), F32),
            pltpu.VMEM((NY - 1, NZ + 1, 8, HW), F32),
            pltpu.VMEM((NZ, 32, HW), F32),
            pltpu.VMEM((NZ - 1, 32, HW), F32),
            pltpu.VMEM((8, 32, HW), F32),
            pltpu.SemaphoreType.DMA((19, 4, 4)),
            pltpu.SemaphoreType.DMA((19, 4, 4)),
            pltpu.SemaphoreType.DMA((59,)),
            pltpu.SemaphoreType.DMA((59,)),
        ],
        compiler_params=pltpu.CompilerParams(
            collective_id=0, has_side_effects=True, vmem_limit_bytes=58 * 1024 * 1024
        ),
    )(info, hidden, queries, keys, down, direction, up_direction, cosine, sine, up)


def scale_kernel(down_sum, tail, down_out, up_out, curv_out):
    curv_sum = jnp.sum(tail[8:9, :])
    count = jnp.sum(tail[9:10, :])
    rescale = tail[16:17, 0:1] / (curv_sum + 1e-06)
    down_out[...] = down_sum[...] * rescale
    up_out[0:8, :] = tail[0:8, 0:RANK] * rescale
    up_out[8:16, :] = tail[0:8, RANK:HW] * rescale
    curv_out[0, 0] = curv_sum / count


def scaled(down_sum, tail):
    return pl.pallas_call(
        scale_kernel,
        out_shape=(
            jax.ShapeDtypeStruct((RANK, 256), F32),
            jax.ShapeDtypeStruct((16, RANK), F32),
            jax.ShapeDtypeStruct((1, 1), F32),
        ),
        in_specs=[VM, VM],
        out_specs=(VM, VM, SM),
    )(down_sum, tail)


def body(hidden, queries, keys, down, up, direction, up_direction, window, lengths):
    seq = hidden.shape[1]
    span = seq * NZ * NY
    ctx = lax.axis_index("ctx")
    position = window[0] * span + ctx * seq + jnp.arange(seq, dtype=jnp.int32)
    inv_freq = jnp.exp(jnp.arange(HW // 2, dtype=F32) * (-2.0 * math.log(1000000.0) / HW))
    angles = position.astype(F32)[:, None] * inv_freq
    cosine, sine = jnp.cos(angles), jnp.sin(angles)
    info = (lengths - window * span).astype(jnp.int32)
    down_sum, tail = fisher(
        info, hidden[0], queries[0], keys[0], down.T, direction.T, up_direction, cosine, sine, up
    )
    down_out, up_out, curv_out = scaled(down_sum, tail)
    return down_out.T, up_out.T, curv_out[0, 0]


def solution(mesh):
    placed = (
        P("dp", "ctx", None),
        P("dp", "ctx", None),
        P("dp", "ctx", None),
        P(),
        P(),
        P(),
        P(),
        P("dp"),
        P("dp"),
    )
    return jax.shard_map(
        body,
        mesh=mesh,
        in_specs=placed,
        out_specs=(P("ctx", None), P(None, "ctx"), P()),
        check_vma=False,
    )
```

```python
import functools
import math

import jax
import jax.numpy as jnp
from jax import lax
from jax.experimental import pallas as pl
from jax.experimental.pallas import tpu as pltpu
from jax.sharding import PartitionSpec as P

HW = 128
GROUP = 8
RANK = 64
NZ, NY, NX = 8, 4, 4
ROWS = 256
CHUNK = 2048
SUB = 256
F32 = jnp.float32
BF = jnp.bfloat16
MESH = pl.DeviceIdType.MESH
NN = (((1,), (0,)), ((), ()))
NT = (((1,), (1,)), ((), ()))
VM = pl.BlockSpec(memory_space=pltpu.VMEM)
SM = pl.BlockSpec(memory_space=pltpu.SMEM)


def dot(a, b, dims=NN):
    return lax.dot_general(a, b, dims, preferred_element_type=F32)


def place():
    ctx = lax.axis_index("ctx")
    return ctx // NY, lax.rem(ctx, NY)


def forward(size):
    steps = [[(-k, 1, None), (k, -1, None)] for k in range(size // 2 - 1)]
    last = size // 2 - 1
    return steps + [[(-last, 1, 0), (last, -1, 1)]]


DIRECT4 = [[(0, 1, None), (0, -1, None), (0, 2, None)]]
THREE8 = [
    [(0, 1, None), (0, -1, None)],
    [(-1, 1, None), (1, -1, None)],
    [(-2, 1, None), (2, -1, None), (-2, 2, 0), (2, -2, 1)],
]
TWO8 = [
    [(0, 1, None), (0, -1, None), (0, 2, None), (0, -2, None)],
    [(-2, 1, None), (2, -1, None), (-2, 2, 0), (2, -2, 1)],
]


class Flow:
    def __init__(self, index, size, here, plan, block, peer, sems):
        self.index, self.size, self.here, self.plan = index, size, here, plan
        self.block, self.peer = block, peer
        self.send_sem, self.recv_sem = sems
        self.step = -1

    def copy(self, step, k, arriving):
        held, hop, half = self.plan[step][k]
        origin = held - hop if arriving else held
        ref = self.block(lax.rem(self.here + origin + 2 * self.size, self.size), half)
        return pltpu.make_async_remote_copy(
            src_ref=ref,
            dst_ref=ref,
            send_sem=self.send_sem.at[self.index, step, k],
            recv_sem=self.recv_sem.at[self.index, step, k],
            device_id=self.peer(lax.rem(self.here + hop + self.size, self.size)),
            device_id_type=MESH,
        )

    def send(self, step):
        self.step = step
        for k in range(len(self.plan[step])):
            self.copy(step, k, False).start()

    def receive(self, step):
        for k in range(len(self.plan[step])):
            self.copy(step, k, True).wait_recv()
        return sorted({(held - hop) % self.size for held, hop, _ in self.plan[step]})

    def advance(self):
        step = self.step
        came = self.receive(step)
        end = step + 1 == len(self.plan)
        if not end:
            self.send(step + 1)
        return came, end

    def drain(self):
        for step, moves in enumerate(self.plan):
            for k in range(len(moves)):
                self.copy(step, k, False).wait_send()


def cut(ref, half, axis):
    if half is None:
        return ref
    return ref.at[(slice(None),) * axis + (pl.ds(half * 64, 64),)]


def fisher_kernel(
    info, hidden_any, queries_any, keys, down_any, direction_any, up_direction, cosine, sine, up,
    down_out, tail_out,
    hidden, queries, down, direction, load_sem, wT,
    gath, qT, s_even, s_odd, p_even, p_odd, vT, act, grad, oacc, w_even, w_odd, curv_acc, mixed, upT,
    got_y, sum_y, got_z, part, got_core, sum_core, got_xy, ups, got_uy, sum_dy, got_dz, all_dp,
    gsend, grecv, send_sem, recv_sem,
):
    z, y = place()
    dp = lax.axis_index("dp")
    x, core = dp // 2, lax.rem(dp, 2)
    loads = [
        pltpu.make_async_copy(src, dst, load_sem.at[k])
        for k, (src, dst) in enumerate(
            ((hidden_any, hidden), (down_any, down), (direction_any, direction), (queries_any, queries))
        )
    ]
    for copy in loads:
        copy.start()
    barrier = pltpu.get_barrier_semaphore()

    def at(zz, yy):
        return {"ctx": zz * NY + yy}

    def at_y(o):
        return {"ctx": z * NY + lax.rem(y + o, NY)}

    def at_z(o):
        return {"ctx": lax.rem(z + o, NZ) * NY + y}

    def at_dp(o):
        return {"dp": lax.rem(dp + o, 8)}

    def at_xy(ox, oy):
        return {"dp": lax.rem(x + ox, NX) * 2 + core, "ctx": z * NY + lax.rem(y + oy, NY)}

    plane = [(ox, oy) for ox in range(NX) for oy in range(NY) if ox or oy]
    for ox, oy in plane:
        pl.semaphore_signal(barrier, inc=1, device_id=at_xy(ox, oy), device_id_type=MESH)
    for o in range(1, NZ):
        pl.semaphore_signal(barrier, inc=1, device_id=at_z(o), device_id_type=MESH)
    for o in range(NX):
        other = {"dp": lax.rem(x + o, NX) * 2 + 1 - core}
        pl.semaphore_signal(barrier, inc=1, device_id=other, device_id_type=MESH)

    ys = [lax.rem(y + o, NY) for o in range(NY)]
    zs = [lax.rem(z + o, NZ) for o in range(NZ)]
    cos = jnp.concatenate([cosine[...], cosine[...]], axis=1)
    sin = jnp.concatenate([-sine[...], sine[...]], axis=1)

    def turn(u):
        u = u.astype(F32)
        return u * cos + pltpu.roll(u, HW // 2, 1) * sin

    for g in range(4):
        gath[1 + g, z, y] = turn(keys[:, g * HW : (g + 1) * HW]).astype(BF)
    pl.semaphore_wait(barrier, 26)

    made = []
    sems = (gsend, grecv)

    def ring_y(plan, block):
        made.append(Flow(len(made), NY, y, plan, block, lambda to: at(z, to), sems))
        return made[-1]

    def ring_z(plan, block):
        made.append(Flow(len(made), NZ, z, plan, block, lambda to: at(to, y), sems))
        return made[-1]

    def y_lane(head, zz, plan):
        return ring_y(plan, lambda o, half: cut(gath.at[head, zz, o], half, 0))

    def z_lane(head, yy, plan):
        return ring_z(plan, lambda o, half: cut(gath.at[head, o, yy], half, 0))

    def y_rest(head):
        return ring_y(forward(NY), lambda o, half: cut(gath.at[head, :, o], half, 1))

    first_z = z_lane(1, y, TWO8)
    key_lanes = [y_lane(1, z, forward(NY))]
    for flow in (first_z, key_lanes[0]):
        flow.send(0)
    for copy in loads[:3]:
        copy.wait()
    gath[0, z, y, 0:RANK, :] = dot(down[...], hidden[...], NT).astype(BF)
    gath[0, z, y, RANK:HW, :] = dot(direction[...], hidden[...], NT).astype(BF)
    first_y = y_lane(0, z, DIRECT4)
    act_lanes = {0: z_lane(0, y, forward(NZ))}
    for flow in (first_y, act_lanes[0]):
        flow.send(0)

    loads[3].wait()
    scale = math.log2(math.e) / math.sqrt(HW)

    def rotate_queries(i, _):
        for h in range(ROWS // HW):
            u = queries[:, pl.ds(pl.multiple_of(i * ROWS + h * HW, HW), HW)]
            qT[i, :, h * HW : (h + 1) * HW] = jnp.transpose(turn(u) * scale).astype(BF)
        return 0

    def rotate_some(k):
        lax.fori_loop(4 * k, 4 * k + 4, rotate_queries, 0)

    for g in range(4):
        cols = slice(g * HW, (g + 1) * HW)
        block = jnp.concatenate([up_direction[:, cols], up[:, cols]], axis=0).astype(F32)
        wT[cols, :] = jnp.transpose(block).astype(BF)

    kvh = 4
    blocks = NZ * NY
    span = blocks * HW
    per = CHUNK // HW
    me, live = z * NY + y, info[0]
    chunks = me // per + 1
    per_g = GROUP * HW // ROWS
    total = kvh * per_g
    zper = per // NY

    def tangents(zz, yy):
        cols = pl.ds(pl.multiple_of((zz * NY + yy) * HW, HW), HW)
        vv = dot(wT[...], gath[0, zz, yy]).astype(BF)
        for g in range(kvh):
            vT[g, 0:HW, cols] = vv[g * HW : (g + 1) * HW]
        act[:, cols] = gath[0, zz, yy, 0:RANK, :]

    tangents(z, y)
    ones = jnp.where(lax.broadcasted_iota(jnp.int32, (16, span), 0) == 0, 1.0, 0.0).astype(BF)
    for g in range(kvh):
        vT[g, HW : HW + 16, :] = ones
    grad[...] = jnp.zeros_like(grad)
    curv_acc[...] = jnp.zeros_like(curv_acc)
    rotate_some(0)

    s_bufs, p_bufs, w_bufs = (s_even, s_odd), (p_even, p_odd), (w_even, w_odd)
    qpos = me * HW + lax.rem(lax.broadcasted_iota(jnp.int32, (1, ROWS), 1), HW)
    liverow = (qpos < live).astype(F32)

    def step(i, even, score, weigh, back, m_prev):
        odd = 1 - even
        if weigh:
            oacc[...] = jnp.zeros_like(oacc)
        q = qT[i] if score else None

        def body(j, mx):
            o = None
            for u in range(CHUNK // SUB):
                us = pl.multiple_of(j * CHUNK + u * SUB, SUB)
                if back:
                    grad[(i - 2) // per_g, :, pl.ds(us, SUB)] += dot(
                        w_bufs[even][...], p_bufs[even][pl.ds(us, SUB), :], NT
                    )
                if score:
                    b = u * (SUB // HW)
                    kc = gath[1 + i // per_g, j * zper + b // NY, b % NY : b % NY + SUB // HW].reshape(SUB, HW)
                    s = dot(kc, q)
                    kpos = us + lax.broadcasted_iota(jnp.int32, (SUB, ROWS), 0)
                    s = jnp.where(kpos <= qpos, s, -1e30)
                    s_bufs[even][pl.ds(us, SUB), :] = s
                    mx = jnp.maximum(mx, jnp.max(s.reshape(SUB // 8, 8, ROWS), axis=0))
                if weigh:
                    p = jnp.exp2(s_bufs[odd][pl.ds(us, SUB), :] - m_prev).astype(BF)
                    p_bufs[odd][pl.ds(us, SUB), :] = p
                    t = dot(vT[(i - 1) // per_g, :, pl.ds(us, SUB)], p)
                    o = t if o is None else o + t
            if weigh:
                oacc[...] += o
            return mx

        mx = lax.fori_loop(0, chunks, body, jnp.full((8, ROWS), -1e30, F32))
        if weigh:
            o = oacc[...]
            inv = 1.0 / o[HW : HW + 1]
            out = o[0:HW] * inv * liverow
            curv_acc[...] += jnp.sum((out * out).reshape(HW // 8, 8, ROWS), axis=0)
            w_bufs[odd][...] = (out * inv).astype(BF)
        return jnp.max(mx, axis=0, keepdims=True)

    for slot in range(1, 5):
        new_keys, new_acts, landed = [], {}, []
        if slot <= 2:
            came, _ = first_z.advance()
            new_keys = [y_lane(1, zs[o], forward(NY) if slot == 1 else DIRECT4) for o in came]
            for flow in new_keys:
                flow.send(0)
        if slot == 1:
            came, _ = first_y.advance()
            new_acts = {o: z_lane(0, ys[o], THREE8) for o in came}
            landed += [(0, o) for o in came]
        for o, flow in list(act_lanes.items()):
            came, end = flow.advance()
            landed += [(oz, o) for oz in came]
            if end:
                del act_lanes[o]
        for flow in new_acts.values():
            flow.send(0)
        act_lanes.update(new_acts)
        for flow in list(key_lanes):
            if flow.advance()[1]:
                key_lanes.remove(flow)
        key_lanes += new_keys
        if slot == 1:
            keys1_z = z_lane(2, y, TWO8)
            keys1_z.send(0)
        if slot == 2:
            keys1_z.advance()
        if slot == 3:
            keys1_z.advance()
            keys1_y = y_rest(2)
            keys1_y.send(0)
            keys2_y = y_lane(3, z, DIRECT4)
            keys2_y.send(0)
        if slot == 4:
            keys2_y.receive(0)
            keys2_z = ring_z(forward(NZ), lambda o, half: cut(gath.at[3, o], half, 1))
            keys2_z.send(0)
            keys3_z = z_lane(4, y, TWO8)
            keys3_z.send(0)
            keys3_y = y_rest(4)
        if slot < 4:
            rotate_some(slot)
        for oz, oy in landed:
            tangents(zs[oz], ys[oy])
        if slot == 3:
            top = step(0, 0, True, False, False, None)

    def pass_on(flow, step, then=None):
        def act():
            flow.receive(step)
            if then is not None:
                then[0].send(then[1])

        return act

    hooks = {
        2: [pass_on(keys1_y, 0, (keys1_y, 1)), pass_on(keys2_z, 0, (keys2_z, 1))],
        3: [pass_on(keys3_z, 0, (keys3_z, 1))],
        4: [pass_on(keys1_y, 1), pass_on(keys2_z, 1, (keys2_z, 2))],
        5: [pass_on(keys3_z, 1, (keys3_y, 0))],
        6: [pass_on(keys2_z, 2, (keys2_z, 3))],
        8: [pass_on(keys2_z, 3)],
        9: [pass_on(keys3_y, 0, (keys3_y, 1))],
        12: [pass_on(keys3_y, 1)],
    }

    def serve(i, odd):
        for n, acts in hooks.items():
            if n % 2 == odd:

                @pl.when(i == n // 2)
                def _():
                    for act in acts:
                        act()

    top = step(1, 1, True, True, False, top)

    def pair(i, top):
        serve(i, 0)
        top = step(2 * i, 0, True, True, True, top)
        serve(i, 1)
        return step(2 * i + 1, 1, True, True, True, top)

    top = lax.fori_loop(1, total // 2, pair, top)
    step(total, 0, False, True, True, top)
    step(total + 1, 1, False, False, True, None)

    used = [0]
    sent = []

    def send(src, dst, to):
        copy = pltpu.make_async_remote_copy(
            src_ref=src, dst_ref=dst, send_sem=send_sem.at[used[0]], recv_sem=recv_sem.at[used[0]],
            device_id=to, device_id_type=MESH,
        )
        used[0] += 1
        copy.start()
        sent.append(copy)
        return copy

    mixed[...] = jnp.zeros_like(mixed)
    upT[...] = jnp.zeros_like(upT)

    def mix(j, _):
        ks = pl.multiple_of(j * CHUNK, CHUNK)
        acc = sum(
            dot(up[:, g * HW : (g + 1) * HW], grad[g, :, pl.ds(ks, CHUNK)].astype(BF)) for g in range(kvh)
        ).astype(BF)
        for b in range(per):
            mixed[j * zper + b // NY, b % NY] = acc[:, b * HW : (b + 1) * HW]
        return 0

    lax.fori_loop(0, chunks, mix, 0)

    copies = [
        send(mixed.at[:, lax.rem(y + o, NY)], got_y.at[o - 1], at_y(o)) for o in range(1, NY)
    ]

    def ascend(j, _):
        ks = pl.multiple_of(j * CHUNK, CHUNK)
        for g in range(kvh):
            upT[g * HW : (g + 1) * HW, :] += dot(
                grad[g, :, pl.ds(ks, CHUNK)].astype(BF), act[:, pl.ds(ks, CHUNK)], NT
            )
        return 0

    lax.fori_loop(0, chunks, ascend, 0)
    both = curv_acc[:, 0:HW] + curv_acc[:, HW : 2 * HW]
    row = lax.broadcasted_iota(jnp.int32, (8, HW), 0)
    lane = lax.broadcasted_iota(jnp.int32, (8, HW), 1)
    mine = ((me * HW + lane) < live).astype(F32)
    curv = jnp.where(
        row == 0, jnp.sum(both, axis=0, keepdims=True), jnp.where(row == 1, mine, 0.0)
    )
    for i in range(32):
        block = upT[16 * i : 16 * i + 16, :]
        ups[i % NY, i // NY] = jnp.concatenate([block[0:8], block[8:16]], axis=1)
    for i in range(NY):
        ups[i, NZ] = curv

    def squares(i, acc):
        d = direction[:, pl.ds(pl.multiple_of(i * 512, 512), 512)].astype(F32)
        return acc + jnp.sum((d * d).reshape(8, 8, 512), axis=0)

    squared = jnp.sum(lax.fori_loop(0, 16, squares, jnp.zeros((8, 512), F32)))
    ud = up_direction[...].astype(F32)
    squared = squared + jnp.sum(ud * ud)

    for copy in copies:
        copy.wait_recv()

    def add_y(i, _):
        acc = mixed[i, y].astype(F32)
        for o in range(NY - 1):
            acc = acc + got_y[o, i].astype(F32)
        sum_y[i] = acc.astype(BF)
        return 0

    lax.fori_loop(0, NZ, add_y, 0)
    copies = [
        send(sum_y.at[lax.rem(z + o, NZ)], got_z.at[o - 1], at_z(o)) for o in range(1, NZ)
    ]
    for copy in copies:
        copy.wait_recv()
    own = sum_y[z].astype(F32)
    for o in range(NZ - 1):
        own = own + got_z[o].astype(F32)
    own = own.astype(BF)

    def make_down(h):
        def down_block(i, _):
            for u in range(2):
                k = 2 * i + u
                d = dot(own, hidden[:, pl.ds(pl.multiple_of((h * 16 + k) * 256, 256), 256)])
                for r in range(8):
                    rows = d[8 * r : 8 * r + 8]
                    part[h, r // 2, r % 2, k] = jnp.concatenate([rows[:, 0:HW], rows[:, HW:]], axis=0).astype(BF)
            return 0

        lax.fori_loop(0, 8, down_block, 0)
        return send(part.at[h, :, 1 - core], got_core.at[h], {"dp": x * 2 + 1 - core})

    def add_core(h):
        def add(i, _):
            for xx in range(NX):
                sum_core[h, xx, i % NY, i // NY] = (
                    part[h, xx, core, i].astype(F32) + got_core[h, xx, i].astype(F32)
                ).astype(BF)
            return 0

        lax.fori_loop(0, 16, add, 0)
        return [
            send(
                sum_core.at[h, lax.rem(x + ox, NX), lax.rem(y + oy, NY)], got_xy.at[h, k], at_xy(ox, oy)
            )
            for k, (ox, oy) in enumerate(plane)
        ]

    cores = [make_down(0), make_down(1)]
    cores[0].wait_recv()
    first = add_core(0)
    up_copies = [send(ups.at[lax.rem(y + o, NY)], got_uy.at[o - 1], at_y(o)) for o in range(1, NY)]
    cores[1].wait_recv()
    second = add_core(1)
    for h, copies in ((0, first), (1, second)):
        for copy in copies:
            copy.wait_recv()
        for i in range(NZ // 2):
            acc = sum_core[h, x, y, i].astype(F32)
            for k in range(len(plane)):
                acc = acc + got_xy[h, k, i].astype(F32)
            sum_dy[h * (NZ // 2) + i, 0:16] = acc
    for copy in up_copies:
        copy.wait_recv()
    scal = ups[y, NZ]
    for o in range(NY - 1):
        scal = scal + got_uy[o, NZ]
    for i in range(NZ):
        upa = ups[y, i]
        for o in range(NY - 1):
            upa = upa + got_uy[o, i]
        sum_dy[i, 16:24] = upa
        sum_dy[i, 24:32] = scal
    copies = [
        send(sum_dy.at[lax.rem(z + o, NZ)], got_dz.at[o - 1], at_z(o)) for o in range(1, NZ)
    ]
    for copy in copies:
        copy.wait_recv()
    acc = sum_dy[z]
    for o in range(NZ - 1):
        acc = acc + got_dz[o]
    all_dp[dp] = acc
    copies = [send(all_dp.at[dp], all_dp.at[dp], at_dp(o)) for o in range(1, 8)]
    for o in range(1, 8):
        slot = lax.rem(dp + 8 - o, 8)
        base = used[0] - 7 + o - 1
        pltpu.make_async_remote_copy(
            src_ref=all_dp.at[slot], dst_ref=all_dp.at[slot], send_sem=send_sem.at[base],
            recv_sem=recv_sem.at[base], device_id=at_dp(o), device_id_type=MESH,
        ).wait_recv()
    tail = all_dp[0, 16:32]
    for r in range(1, 8):
        tail = tail + all_dp[r, 16:32]
    for r in range(8):
        down_out[8 * r : 8 * r + 8, 0:HW] = all_dp[r, 0:8]
        down_out[8 * r : 8 * r + 8, HW : 2 * HW] = all_dp[r, 8:16]
    tail_out[0:16, :] = tail
    tail_out[16:24, :] = jnp.full((8, HW), squared, F32)
    for flow in made:
        flow.drain()
    for copy in sent:
        copy.wait_send()


def fisher(info, hidden, queries, keys, down, direction, up_direction, cosine, sine, up):
    span = NZ * NY * HW
    half = NZ // 2
    anywhere = pl.BlockSpec(memory_space=pl.ANY)
    return pl.pallas_call(
        fisher_kernel,
        out_shape=(
            jax.ShapeDtypeStruct((RANK, 256), F32),
            jax.ShapeDtypeStruct((24, HW), F32),
        ),
        in_specs=[SM, anywhere, anywhere, VM, anywhere, anywhere, VM, VM, VM, VM],
        out_specs=(VM, VM),
        scratch_shapes=[
            pltpu.VMEM(hidden.shape, BF),
            pltpu.VMEM(queries.shape, BF),
            pltpu.VMEM(down.shape, BF),
            pltpu.VMEM(direction.shape, BF),
            pltpu.SemaphoreType.DMA((4,)),
            pltpu.VMEM((4 * HW, HW), BF),
            pltpu.VMEM((5, NZ, NY, HW, HW), BF),
            pltpu.VMEM((queries.shape[1] // ROWS, HW, ROWS), BF),
            pltpu.VMEM((span, ROWS), F32),
            pltpu.VMEM((span, ROWS), F32),
            pltpu.VMEM((span, ROWS), BF),
            pltpu.VMEM((span, ROWS), BF),
            pltpu.VMEM((4, HW + 16, span), BF),
            pltpu.VMEM((RANK, span), BF),
            pltpu.VMEM((4, HW, span), F32),
            pltpu.VMEM((HW + 16, ROWS), F32),
            pltpu.VMEM((HW, ROWS), BF),
            pltpu.VMEM((HW, ROWS), BF),
            pltpu.VMEM((8, ROWS), F32),
            pltpu.VMEM((NZ, NY, RANK, HW), BF),
            pltpu.VMEM((4 * HW, RANK), F32),
            pltpu.VMEM((NY - 1, NZ, RANK, HW), BF),
            pltpu.VMEM((NZ, RANK, HW), BF),
            pltpu.VMEM((NZ - 1, RANK, HW), BF),
            pltpu.VMEM((2, NX, 2, 16, 16, HW), BF),
            pltpu.VMEM((2, NX, 16, 16, HW), BF),
            pltpu.VMEM((2, NX, NY, half, 16, HW), BF),
            pltpu.VMEM((2, NX * NY - 1, half, 16, HW), BF),
            pltpu.VMEM((NY, NZ + 1, 8, HW), F32),
            pltpu.VMEM((NY - 1, NZ + 1, 8, HW), F32),
            pltpu.VMEM((NZ, 32, HW), F32),
            pltpu.VMEM((NZ - 1, 32, HW), F32),
            pltpu.VMEM((8, 32, HW), F32),
            pltpu.SemaphoreType.DMA((20, 4, 4)),
            pltpu.SemaphoreType.DMA((20, 4, 4)),
            pltpu.SemaphoreType.DMA((59,)),
            pltpu.SemaphoreType.DMA((59,)),
        ],
        compiler_params=pltpu.CompilerParams(
            collective_id=0, has_side_effects=True, vmem_limit_bytes=58 * 1024 * 1024
        ),
    )(info, hidden, queries, keys, down, direction, up_direction, cosine, sine, up)


def scale_kernel(down_sum, tail, down_out, up_out, curv_out):
    curv_sum = jnp.sum(tail[8:9, :])
    count = jnp.sum(tail[9:10, :])
    rescale = tail[16:17, 0:1] / (curv_sum + 1e-06)
    down_out[...] = down_sum[...] * rescale
    up_out[0:8, :] = tail[0:8, 0:RANK] * rescale
    up_out[8:16, :] = tail[0:8, RANK:HW] * rescale
    curv_out[0, 0] = curv_sum / count


def scaled(down_sum, tail):
    return pl.pallas_call(
        scale_kernel,
        out_shape=(
            jax.ShapeDtypeStruct((RANK, 256), F32),
            jax.ShapeDtypeStruct((16, RANK), F32),
            jax.ShapeDtypeStruct((1, 1), F32),
        ),
        in_specs=[VM, VM],
        out_specs=(VM, VM, SM),
    )(down_sum, tail)


def body(hidden, queries, keys, down, up, direction, up_direction, window, lengths):
    seq = hidden.shape[1]
    span = seq * NZ * NY
    ctx = lax.axis_index("ctx")
    position = window[0] * span + ctx * seq + jnp.arange(seq, dtype=jnp.int32)
    inv_freq = jnp.exp(jnp.arange(HW // 2, dtype=F32) * (-2.0 * math.log(1000000.0) / HW))
    angles = position.astype(F32)[:, None] * inv_freq
    cosine, sine = jnp.cos(angles), jnp.sin(angles)
    info = (lengths - window * span).astype(jnp.int32)
    down_sum, tail = fisher(
        info, hidden[0], queries[0], keys[0], down.T, direction.T, up_direction, cosine, sine, up
    )
    down_out, up_out, curv_out = scaled(down_sum, tail)
    return down_out.T, up_out.T, curv_out[0, 0]


def solution(mesh):
    placed = (
        P("dp", "ctx", None),
        P("dp", "ctx", None),
        P("dp", "ctx", None),
        P(),
        P(),
        P(),
        P(),
        P("dp"),
        P("dp"),
    )
    return jax.shard_map(
        body,
        mesh=mesh,
        in_specs=placed,
        out_specs=(P("ctx", None), P(None, "ctx"), P()),
        check_vma=False,
    )
```
